256 devices in a mesh: ctx: 32 (over y_hi, z, core), tp: 8 (over y_lo, x).
Axes of the slice: x: 4, y: 4 (y_hi: 2, y_lo: 2; y = y_hi * 2 + y_lo), z: 8, core: 2. Of those that a mesh axis runs over, the one named last changes fastest.
Arguments:
- query_heads: bfloat16 [4096, 8192], P('ctx', 'tp'), may hold values from -32 to 32
- key_heads: bfloat16 [4096, 8192], P('ctx', 'tp'), may hold values from -6 to 6
- value_heads: bfloat16 [4096, 8192], P('ctx', 'tp'), may hold values from -6 to 6
- hyena_query: bfloat16 [4096, 8192], P('ctx', 'tp'), may hold values from -6 to 6
- hyena_key: bfloat16 [4096, 8192], P('ctx', 'tp'), may hold values from -6 to 6
- hyena_value: bfloat16 [4096, 8192], P('ctx', 'tp'), may hold values from -6 to 6
- short_filter: float32 [3, 7, 8192], P(None, None, 'tp'), may hold values from -2 to 2
- long_filter: float32 [4096, 512], P('ctx', 'tp'), may hold values from -0.09375 to 0.09375
- output_grad: bfloat16 [4096, 8192], P('ctx', 'tp'), may hold values from -70 to 70
Outputs:
- attention: bfloat16 [4096, 8192], P('ctx', 'tp')
- query_grad: bfloat16 [4096, 8192], P('ctx', 'tp')
- key_grad: bfloat16 [4096, 8192], P('ctx', 'tp')
- value_grad: bfloat16 [4096, 8192], P('ctx', 'tp')
- filter_grad: float32 [4096, 512], P('ctx', 'tp')
The draws below stay inside these ranges and needn't reach their ends.
All inputs are finite; a program needn't handle non-finite values.
Results may differ from the reference program's by a relative error of at most 0.0049.
Values may be sent and summed in bfloat16 or wider, within the bound.
A program may use at most 64 MiB of HBM per device.

```python
import math
import jax
import jax.numpy as jnp
from jax import lax

HEADS = 64
HEAD_DIM = 128
GROUPS = 512
TOK_DEV = 128
SHORT = 7
D = 8192
SEQ = 4096


def draw_pair(key):
    key_query, key_key = jax.random.split(jax.random.fold_in(key, 17), 2)
    queries = jnp.clip(jax.random.normal(key_query, (SEQ, D), jnp.float32), -6.0, 6.0)
    keys = jnp.clip(jax.random.normal(key_key, (SEQ, D), jnp.float32), -6.0, 6.0)
    return (queries, keys)


def draw_query_heads(key, part):
    return draw_pair(key)[0].astype(jnp.bfloat16)


def draw_key_heads(key, part):
    return draw_pair(key)[1].astype(jnp.bfloat16)


def draw_output_grad(key, part):
    key_noise, key_scale = jax.random.split(jax.random.fold_in(key, 29), 2)
    column = jnp.arange(D).astype(jnp.float32) / D
    jitter = jax.random.uniform(key_scale, (D,), jnp.float32)
    spread = jnp.exp(math.log(10.0) * (0.5 * column + 0.5 * jitter))
    noise = jnp.clip(jax.random.normal(key_noise, (SEQ, D), jnp.float32), -4.0, 4.0)
    values = noise * spread[None, :]
    return values.astype(jnp.bfloat16)


def block_scale(stream_key, dims, shards, smallest, top_value):
    def one(axis_at, blocks):
        heights = jax.random.uniform(jax.random.fold_in(jax.random.fold_in(stream_key, 6), axis_at), (blocks,), jnp.float32, smallest / len(shards), top_value / len(shards))
        return jnp.repeat(jnp.exp(heights), dims[axis_at] // blocks).reshape((-1,) + (1,) * (len(dims) - axis_at - 1))

    level = one(*shards[0])
    for cut in shards[1:]:
        level = level * one(*cut)
    return level


def gaussian(own_key, extent, scale, reach, pieces=(), kind=jnp.bfloat16):
    values = jax.random.normal(own_key, extent, jnp.float32) * scale
    if len(pieces) > 0:
        values = block_scale(own_key, extent, pieces, -0.22, 0.18) * values
    return jnp.clip(values, min=-reach, max=reach).astype(kind)


def setup_inputs(seed: int = 0) -> dict:
    arg_keys = jax.random.split(jax.random.key(seed), 10)
    query_heads = draw_query_heads(jax.random.fold_in(arg_keys[9], 71), 0)
    key_heads = draw_key_heads(jax.random.fold_in(arg_keys[9], 71), 0)
    value_heads = gaussian(arg_keys[2], (SEQ, D), 1.0, 6.0, ((0, 32), (1, 8)))
    hyena_query = gaussian(arg_keys[3], (SEQ, D), 1.0, 6.0, ((0, 32), (1, 8)))
    hyena_key = gaussian(arg_keys[4], (SEQ, D), 1.0, 6.0, ((0, 32), (1, 8)))
    hyena_value = gaussian(arg_keys[5], (SEQ, D), 1.0, 6.0, ((0, 32), (1, 8)))
    short_filter = gaussian(arg_keys[6], (3, SHORT, D), SHORT ** -0.5, 2.0, ((2, 8),), jnp.float32)
    long_filter = gaussian(arg_keys[7], (SEQ, GROUPS), SEQ ** -0.5, 0.09375, ((0, 32), (1, 8)), jnp.float32)
    output_grad = draw_output_grad(jax.random.fold_in(arg_keys[9], 71), 0)
    return {"query_heads": query_heads, "key_heads": key_heads, "value_heads": value_heads, "hyena_query": hyena_query, "hyena_key": hyena_key, "hyena_value": hyena_value, "short_filter": short_filter, "long_filter": long_filter, "output_grad": output_grad}


def attend_blocks(query_heads, key_heads, value_heads):
    blocks = SEQ // TOK_DEV
    queries = query_heads.astype(jnp.float32).reshape(SEQ, HEADS, HEAD_DIM)
    padding = jnp.zeros((TOK_DEV, HEADS, HEAD_DIM), jnp.float32)
    keys_padded = jnp.concatenate([padding, key_heads.astype(jnp.float32).reshape(SEQ, HEADS, HEAD_DIM)], 0)
    values_padded = jnp.concatenate([padding, value_heads.astype(jnp.float32).reshape(SEQ, HEADS, HEAD_DIM)], 0)

    def single(block):
        start = (block * TOK_DEV).astype(jnp.int32)
        query_rows = lax.dynamic_slice_in_dim(queries, start, TOK_DEV, 0)
        key_rows = lax.dynamic_slice_in_dim(keys_padded, start, 2 * TOK_DEV, 0)
        value_rows = lax.dynamic_slice_in_dim(values_padded, start, 2 * TOK_DEV, 0)
        scores = jnp.einsum('qhd,khd->hqk', query_rows, key_rows) * (1.0 / math.sqrt(HEAD_DIM))
        query_pos = start + jnp.arange(TOK_DEV, dtype=jnp.int32)[:, None]
        key_pos = start - TOK_DEV + jnp.arange(2 * TOK_DEV, dtype=jnp.int32)[None, :]
        allowed = (key_pos <= query_pos) & (key_pos >= 0)
        masked = jnp.where(allowed[None], scores, -jnp.inf)
        largest = lax.optimization_barrier(jnp.max(masked, axis=2, keepdims=True))
        raised = jnp.exp(masked - largest)
        weights = (raised / lax.optimization_barrier(jnp.sum(raised, axis=2, keepdims=True))).astype(jnp.bfloat16)
        mixed = jnp.einsum('hqk,khd->qhd', weights.astype(jnp.float32), value_rows)
        return mixed.astype(jnp.bfloat16)
    result = lax.map(single, jnp.arange(blocks, dtype=jnp.int32))
    return result.reshape(SEQ, HEADS * HEAD_DIM)

def causal_short(signal, filter_taps):
    padded = jnp.concatenate([jnp.zeros((SHORT - 1, D), jnp.float32), signal], 0)
    total = jnp.zeros((SEQ, D), jnp.float32)
    for offset in range(SHORT):
        total = total + filter_taps[offset] * padded[SHORT - 1 - offset:SHORT - 1 - offset + SEQ]
    return total

def anti_short(signal, filter_taps):
    padded = jnp.concatenate([signal, jnp.zeros((SHORT - 1, D), jnp.float32)], 0)
    total = jnp.zeros((SEQ, D), jnp.float32)
    for offset in range(SHORT):
        total = total + filter_taps[offset] * padded[offset:offset + SEQ]
    return total

def long_products(mixed, filter_taps, delta):
    group = math.gcd(D, 512)
    count = D // group
    stacked = jnp.stack([mixed, filter_taps, delta]).reshape(3, SEQ, count, group).transpose(2, 0, 1, 3)

    def one_group(signals):
        spectra = jnp.fft.rfft(signals, n=2 * SEQ, axis=1)
        mixed_spec, filter_spec, delta_spec = (spectra[0], spectra[1], spectra[2])
        conv = jnp.fft.irfft(filter_spec * mixed_spec, n=2 * SEQ, axis=0)[:SEQ]
        grad_mixed = jnp.fft.irfft(jnp.conj(filter_spec) * delta_spec, n=2 * SEQ, axis=0)[:SEQ]
        raw_grad = jnp.fft.irfft(jnp.conj(mixed_spec) * delta_spec, n=2 * SEQ, axis=0)[:SEQ]
        return jnp.stack([conv, grad_mixed, raw_grad]).astype(jnp.float32)
    result = lax.map(one_group, stacked)
    result = result.transpose(1, 2, 0, 3).reshape(3, SEQ, D)
    return (result[0], result[1], result[2])

def reference(query_heads, key_heads, value_heads, hyena_query, hyena_key, hyena_value, short_filter, long_filter, output_grad):
    attention = attend_blocks(query_heads, key_heads, value_heads)
    short_q = causal_short(hyena_query.astype(jnp.float32), short_filter[0])
    short_k = causal_short(hyena_key.astype(jnp.float32), short_filter[1])
    short_v = causal_short(hyena_value.astype(jnp.float32), short_filter[2])
    mixed = short_k * short_v
    upstream = output_grad.astype(jnp.float32)
    grad_conv = upstream * short_q
    channel_filter = jnp.repeat(long_filter, D // GROUPS, axis=1)
    conv, grad_mixed, channel_grad = long_products(mixed, channel_filter, grad_conv)
    raw_grad = lax.optimization_barrier(jnp.sum(channel_grad.reshape(SEQ, GROUPS, D // GROUPS), axis=2))
    grad_short_q = upstream * conv
    grad_short_k = grad_mixed * short_v
    grad_short_v = grad_mixed * short_k
    query_grad = anti_short(grad_short_q, short_filter[0]).astype(jnp.bfloat16)
    key_grad = anti_short(grad_short_k, short_filter[1]).astype(jnp.bfloat16)
    value_grad = anti_short(grad_short_v, short_filter[2]).astype(jnp.bfloat16)
    grad_norm = jnp.sqrt(jnp.sum(raw_grad * raw_grad))
    factor = jnp.minimum(1.0, math.sqrt(SEQ * GROUPS) / grad_norm)
    filter_grad = raw_grad * factor
    return (attention, query_grad, key_grad, value_grad, filter_grad)
```

```python
import functools
import math

import jax
import jax.numpy as jnp
from jax import lax
from jax.experimental import pallas as pl
from jax.experimental.pallas import tpu as pltpu
from jax.sharding import PartitionSpec as P

HEAD_DIM = 128
ROWS = 128
CHANNELS = 1024
PEERS = 32
NARROW = 32
GROUP = 16
HELD = 2
TPS = 8
SHORT = 7
RIM = 16
SUPER = 16
LONG = 4096
TOTAL = 4096 * 512
F32 = jnp.float32
BF16 = jnp.bfloat16
MESH = pl.DeviceIdType.MESH


def peer_at(step, me):
    turn = step // 4
    away = ((turn + 1) // 2) * (1 - 2 * (turn % 2)) + 4
    half = 1 - (step // 2) % 2
    core = 1 - step % 2
    return (
        ((me // 16 + half) % 2) * 16 + (((me // 2) % 8 + away) % 8) * 2 + (me % 2 + core) % 2
    )


def dot(a, b, contract):
    return lax.dot_general(a, b, (contract, ((), ())), preferred_element_type=F32)


def kernel(
    q_ref,
    k_ref,
    v_ref,
    hq_ref,
    hk_ref,
    hv_ref,
    taps_ref,
    filt_ref,
    up_ref,
    att_ref,
    qg_ref,
    kg_ref,
    vg_ref,
    fg_ref,
    rim_out,
    rim_in,
    kv_in,
    ext,
    short,
    send_h,
    recv_h,
    send_m,
    recv_m,
    send_g,
    recv_g,
    send_c,
    recv_c,
    send_d,
    recv_d,
    send_f,
    recv_f,
    send_n,
    recv_n,
    edge_out,
    edge_in,
    raw_rows,
    padded_m,
    padded_g,
    left_m,
    left_g,
    weight_c,
    weight_d,
    gram,
    rim_send_sem,
    rim_recv_sem,
    kv_send_sem,
    kv_recv_sem,
    out_sem,
    in_sem,
    edge_send_sem,
    edge_recv_sem,
):
    me = lax.axis_index("ctx")
    tp = lax.axis_index("tp")
    after = (me + 1) % PEERS
    before = (me + PEERS - 1) % PEERS

    barrier = pltpu.get_barrier_semaphore()

    @pl.loop(0, PEERS - 1)
    def _(step):
        pl.semaphore_signal(
            barrier, inc=1, device_id=(peer_at(step, me), tp), device_id_type=MESH
        )

    @pl.loop(1, TPS)
    def _(step):
        pl.semaphore_signal(
            barrier, inc=1, device_id=(me, (tp + step) % TPS), device_id_type=MESH
        )

    rim_out[0:RIM] = hq_ref[ROWS - RIM : ROWS]
    rim_out[RIM : 2 * RIM] = hk_ref[ROWS - RIM : ROWS]
    rim_out[2 * RIM : 3 * RIM] = hv_ref[ROWS - RIM : ROWS]
    filter_first = filt_ref[...].T
    for p in range(PEERS):
        send_h[p] = filter_first[HELD * p : HELD * p + HELD]
    pl.semaphore_wait(barrier, PEERS - 1 + TPS - 1)

    def to_next(src, dst, send_sem, recv_sem, target):
        return pltpu.make_async_remote_copy(
            src_ref=src,
            dst_ref=dst,
            send_sem=send_sem,
            recv_sem=recv_sem,
            device_id=(target, tp),
            device_id_type=MESH,
        )

    rim_copy = to_next(rim_out, rim_in, rim_send_sem, rim_recv_sem, after)
    rim_copy.start()

    def scatter(src, dst, which):
        @pl.loop(0, PEERS - 1)
        def _(step):
            peer = peer_at(step, me)
            to_next(src.at[peer], dst.at[me], out_sem.at[which], in_sem.at[which], peer).start()

        dst[pl.ds(me, 1)] = src[pl.ds(me, 1)]

    def settle(ref, sem):
        part = ref.at[pl.ds(0, PEERS - 1)]
        pltpu.make_async_copy(part, part, sem).wait()

    scatter(send_h, recv_h, 0)
    kv_copies = [
        to_next(src, kv_in.at[n], kv_send_sem.at[n], kv_recv_sem.at[n], after)
        for n, src in enumerate((k_ref, v_ref))
    ]
    for copy in kv_copies:
        copy.start()

    for n, ref in enumerate((hq_ref, hk_ref, hv_ref)):
        ext[n, RIM : RIM + ROWS] = ref[...].astype(F32)
    rim_copy.wait_recv()
    for n in range(3):
        leading = rim_in[n * RIM : (n + 1) * RIM].astype(F32)
        ext[n, 0:RIM] = jnp.where(me > 0, leading, 0.0)

    def short_conv(n, lanes):
        total = taps_ref[n, 0:1, lanes] * ext[n, RIM : RIM + ROWS, lanes]
        for s in range(1, SHORT):
            total += taps_ref[n, s : s + 1, lanes] * ext[n, RIM - s : RIM - s + ROWS, lanes]
        return total

    @pl.loop(0, CHANNELS // 128)
    def _(chunk):
        lanes = pl.ds(pl.multiple_of(chunk * 128, 128), 128)
        short_k = short_conv(1, lanes)
        short_v = short_conv(2, lanes)
        short[1, :, lanes] = short_k
        short[2, :, lanes] = short_v
        mixed = (short_k * short_v).T.astype(BF16)
        send_m[pl.ds(chunk * 4, 4)] = mixed.reshape(4, NARROW, ROWS)

    scatter(send_m, recv_m, 1)

    @pl.loop(0, CHANNELS // 128)
    def _(chunk):
        lanes = pl.ds(pl.multiple_of(chunk * 128, 128), 128)
        delta = (up_ref[:, lanes].astype(F32) * short_conv(0, lanes)).T.astype(BF16)
        send_g[pl.ds(chunk * 4, 4)] = delta.reshape(4, NARROW, ROWS)

    scatter(send_g, recv_g, 2)

    row_at = lax.broadcasted_iota(jnp.int32, (ROWS, ROWS), 0)
    lane_at = lax.broadcasted_iota(jnp.int32, (ROWS, ROWS), 1)
    settle(recv_h, in_sem.at[0])
    zero_tile = jnp.zeros((ROWS, ROWS), BF16)
    for g in range(HELD):
        weight_c[g, 128:256, 0:128] = zero_tile
        weight_d[g, 128:256, 0:128] = zero_tile

        def turned(block, g=g):
            line = jnp.broadcast_to(recv_h[block, g : g + 1], (ROWS, ROWS))
            return pltpu.roll(line, 0, 1, stride=1, stride_axis=0)

        def build(d, last, g=g, turned=turned):
            even = turned(2 * d)
            odd = turned(2 * d + 1)
            tile_even = jnp.where(lane_at >= row_at, even, last).astype(BF16)
            tile_odd = jnp.where(lane_at >= row_at, odd, even).astype(BF16)
            top = pl.multiple_of(d * 256, 256)
            weight_c[g, pl.ds(top, 128), 0:128] = tile_even
            weight_c[g, pl.ds(top + 128, 128), 128:256] = tile_even
            weight_c[g, pl.ds(top, 128), 128:256] = tile_odd
            weight_c[g, pl.ds(top + 384, 128), 0:128] = tile_odd
            weight_d[g, 0:128, pl.ds(top, 128)] = tile_even
            weight_d[g, 128:256, pl.ds(top + 128, 128)] = tile_even
            weight_d[g, 0:128, pl.ds(top + 128, 128)] = tile_odd
            weight_d[g, 128:256, pl.ds(top + 256, 128)] = tile_odd
            return odd

        lax.fori_loop(0, SUPER, build, jnp.zeros((ROWS, ROWS), F32))

    for copy in kv_copies:
        copy.wait_recv()
    query_at = lax.broadcasted_iota(jnp.int32, (ROWS, 2 * ROWS), 0)
    key_at = lax.broadcasted_iota(jnp.int32, (ROWS, 2 * ROWS), 1) - ROWS
    first = jnp.where(me > 0, -ROWS, 0)
    allowed = (key_at <= query_at) & (key_at >= first)

    @pl.loop(0, CHANNELS // HEAD_DIM)
    def _(head):
        lanes = pl.ds(pl.multiple_of(head * HEAD_DIM, HEAD_DIM), HEAD_DIM)
        keys = jnp.concatenate([kv_in[0, :, lanes], k_ref[:, lanes]], 0)
        values = jnp.concatenate([kv_in[1, :, lanes], v_ref[:, lanes]], 0)
        scores = dot(q_ref[:, lanes], keys, ((1,), (1,))) * (1.0 / math.sqrt(HEAD_DIM))
        masked = jnp.where(allowed, scores, -jnp.inf)
        largest = jnp.max(masked, axis=1, keepdims=True)
        raised = jnp.exp(masked - largest)
        weights = (raised / jnp.sum(raised, axis=1, keepdims=True)).astype(BF16)
        att_ref[:, lanes] = dot(weights, values, ((1,), (0,))).astype(BF16)

    half = SUPER * GROUP

    def paired(recv, g):
        rows = recv[:, g * GROUP : (g + 1) * GROUP, :].reshape(SUPER, 2, GROUP, ROWS)
        return rows[:, 0].reshape(half, ROWS), rows[:, 1].reshape(half, ROWS)

    def spread(send, result, g):
        both = jnp.stack(
            [
                result[:, 0:ROWS].reshape(SUPER, GROUP, ROWS),
                result[:, ROWS : 2 * ROWS].reshape(SUPER, GROUP, ROWS),
            ],
            axis=1,
        )
        send[:, g * GROUP : (g + 1) * GROUP, :] = both.reshape(PEERS, GROUP, ROWS)

    settle(recv_m, in_sem.at[1])
    padded_m[0:half] = jnp.zeros((half, 2 * ROWS), BF16)
    for g in range(HELD):
        even, odd = paired(recv_m, g)
        padded_m[half : 2 * half, 0:ROWS] = even
        padded_m[half : 2 * half, ROWS : 2 * ROWS] = odd
        for d in range(SUPER):
            left_m[:, d * 256 : (d + 1) * 256] = padded_m[half - GROUP * d : 2 * half - GROUP * d]
        conv = dot(left_m[...], weight_c[g, 0:LONG], ((1,), (0,))).astype(BF16)
        spread(send_c, conv, g)
    scatter(send_c, recv_c, 3)

    settle(recv_g, in_sem.at[2])
    padded_g[half : 2 * half] = jnp.zeros((half, 2 * ROWS), BF16)
    for g in range(HELD):
        even, odd = paired(recv_g, g)
        padded_g[0:half, 0:ROWS] = even
        padded_g[0:half, ROWS : 2 * ROWS] = odd
        for d in range(SUPER):
            left_g[g, :, d * 256 : (d + 1) * 256] = padded_g[GROUP * d : half + GROUP * d]
        back = dot(left_g[g], weight_d[g, :, 0:LONG], ((1,), (1,))).astype(BF16)
        spread(send_d, back, g)
    scatter(send_d, recv_d, 4)

    reversal = (row_at + lane_at == ROWS - 1).astype(BF16)
    upper = (lane_at < row_at) | (lane_at == ROWS - 1)
    for g in range(HELD):
        turned_m = jnp.concatenate(
            [dot(reversal, part, ((1,), (1,))).astype(BF16) for part in paired(recv_m, g)], 0
        )
        gram[:, 0:LONG] = dot(turned_m, left_g[g], ((1,), (0,)))
        gram[:, LONG : LONG + ROWS] = jnp.zeros((2 * ROWS, ROWS), F32)

        @pl.loop(0, PEERS)
        def _(e, g=g):
            at = pl.multiple_of(e * ROWS, ROWS)
            tile = gram[0:ROWS, pl.ds(at, ROWS)] + gram[ROWS : 2 * ROWS, pl.ds(at + ROWS, ROWS)]
            slid = pltpu.roll(tile, 0, 1, stride=1, stride_axis=0)
            raw_rows[0, pl.ds(e, 1)] = jnp.sum(jnp.where(upper, slid, 0.0), 0, keepdims=True)
            raw_rows[1, pl.ds(e, 1)] = jnp.sum(jnp.where(upper, 0.0, slid), 0, keepdims=True)

        raw_rows[1, PEERS : PEERS + 8] = jnp.zeros((8, ROWS), F32)
        raw = raw_rows[0, 0:PEERS] + raw_rows[1, 1 : PEERS + 1]
        raw = pltpu.roll(raw, 1, 1)
        squares = jnp.sum(raw * raw, 0, keepdims=True)
        send_f[:, g : g + 1, :] = raw.reshape(PEERS, 1, ROWS)
        send_f[:, HELD + g : HELD + g + 1, :] = jnp.broadcast_to(
            squares.reshape(1, 1, ROWS), (PEERS, 1, ROWS)
        )
    scatter(send_f, recv_f, 5)

    def follow(n, source):
        def chunk_step(chunk, carry):
            lanes = pl.ds(pl.multiple_of(chunk * 128, 128), 128)
            part = source[pl.ds(chunk * 4, 4)].reshape(4 * NARROW, ROWS).astype(F32).T
            if n == 0:
                grads = ((0, up_ref[:, lanes].astype(F32) * part),)
            else:
                grads = ((1, part * short[2, :, lanes]), (2, part * short[1, :, lanes]))
            for which, grad in grads:
                ext[which, 0:ROWS, lanes] = grad
                edge_out[which, :, lanes] = grad[0:RIM].astype(BF16)
            return carry

        lax.fori_loop(0, CHANNELS // 128, chunk_step, 0)

    def edge_copy(n):
        part = pl.ds(0, 1) if n == 0 else pl.ds(1, 2)
        return to_next(
            edge_out.at[part],
            edge_in.at[part],
            edge_send_sem.at[n],
            edge_recv_sem.at[n],
            before,
        )

    def anti_short(n, out):
        trailing = edge_in[n].astype(F32)
        ext[n, ROWS : ROWS + RIM] = jnp.where(me < PEERS - 1, trailing, 0.0)

        @pl.loop(0, CHANNELS // 128)
        def _(chunk):
            lanes = pl.ds(pl.multiple_of(chunk * 128, 128), 128)
            total = taps_ref[n, 0:1, lanes] * ext[n, 0:ROWS, lanes]
            for s in range(1, SHORT):
                total += taps_ref[n, s : s + 1, lanes] * ext[n, s : s + ROWS, lanes]
            out[:, lanes] = total.astype(BF16)

    settle(recv_c, in_sem.at[3])
    follow(0, recv_c)
    edge_copy(0).start()
    settle(recv_d, in_sem.at[4])
    follow(1, recv_d)
    edge_copy(1).start()

    settle(recv_f, in_sem.at[5])
    squares = jnp.sum(recv_f[:, HELD : 2 * HELD, :], axis=0)
    squares = jnp.sum(squares, axis=0, keepdims=True)
    send_n[...] = jnp.broadcast_to(squares, (8, ROWS))

    def norm_copy(step):
        return pltpu.make_async_remote_copy(
            src_ref=send_n,
            dst_ref=recv_n.at[tp],
            send_sem=out_sem.at[6],
            recv_sem=in_sem.at[6],
            device_id=(me, (tp + step) % TPS),
            device_id_type=MESH,
        )

    @pl.loop(1, TPS)
    def _(step):
        norm_copy(step).start()

    recv_n[pl.ds(tp, 1)] = send_n[...].reshape(1, 8, ROWS)

    edge_copy(0).wait_recv()
    anti_short(0, qg_ref)
    edge_copy(1).wait_recv()
    anti_short(1, kg_ref)
    anti_short(2, vg_ref)

    part = recv_n.at[pl.ds(0, TPS - 1)]
    pltpu.make_async_copy(part, part, in_sem.at[6]).wait()
    total = jnp.sum(recv_n[:, 0, :], axis=0, keepdims=True)
    total = jnp.sum(total, axis=1, keepdims=True)
    factor = jnp.minimum(1.0, math.sqrt(TOTAL) / jnp.sqrt(total))
    rows = jnp.concatenate([recv_f[p, 0:HELD] for p in range(PEERS)], 0)
    fg_ref[...] = (rows * factor).T

    rim_copy.wait_send()
    for copy in kv_copies:
        copy.wait_send()
    for n in range(2):
        edge_copy(n).wait_send()
    for n, ref in enumerate((send_h, send_m, send_g, send_c, send_d, send_f)):
        settle(ref, out_sem.at[n])
    pltpu.make_async_copy(part, part, out_sem.at[6]).wait()


def on_device(*args):
    vmem = pl.BlockSpec(memory_space=pltpu.VMEM)
    wide = jax.ShapeDtypeStruct((ROWS, CHANNELS), BF16)
    exchanged = pltpu.VMEM((PEERS, NARROW, ROWS), BF16)
    half = SUPER * GROUP
    return pl.pallas_call(
        kernel,
        out_shape=(wide, wide, wide, wide, jax.ShapeDtypeStruct((ROWS, 64), F32)),
        in_specs=[vmem] * 9,
        out_specs=(vmem,) * 5,
        scratch_shapes=[
            pltpu.VMEM((3 * RIM, CHANNELS), BF16),
            pltpu.VMEM((3 * RIM, CHANNELS), BF16),
            pltpu.VMEM((2, ROWS, CHANNELS), BF16),
            pltpu.VMEM((3, ROWS + RIM, CHANNELS), F32),
            pltpu.VMEM((3, ROWS, CHANNELS), F32),
            pltpu.VMEM((PEERS, HELD, ROWS), F32),
            pltpu.VMEM((PEERS, HELD, ROWS), F32),
            *[exchanged] * 8,
            pltpu.VMEM((PEERS, 2 * HELD, ROWS), F32),
            pltpu.VMEM((PEERS, 2 * HELD, ROWS), F32),
            pltpu.VMEM((8, ROWS), F32),
            pltpu.VMEM((TPS, 8, ROWS), F32),
            pltpu.VMEM((3, RIM, CHANNELS), BF16),
            pltpu.VMEM((3, RIM, CHANNELS), BF16),
            pltpu.VMEM((2, PEERS + 8, ROWS), F32),
            pltpu.VMEM((2 * half, 2 * ROWS), BF16),
            pltpu.VMEM((2 * half, 2 * ROWS), BF16),
            pltpu.VMEM((half, LONG), BF16),
            pltpu.VMEM((HELD, half, LONG), BF16),
            pltpu.VMEM((HELD, LONG + 256, 256), BF16),
            pltpu.VMEM((HELD, 256, LONG + 128), BF16),
            pltpu.VMEM((2 * ROWS, LONG + ROWS), F32),
            pltpu.SemaphoreType.DMA,
            pltpu.SemaphoreType.DMA,
            pltpu.SemaphoreType.DMA((2,)),
            pltpu.SemaphoreType.DMA((2,)),
            pltpu.SemaphoreType.DMA((7,)),
            pltpu.SemaphoreType.DMA((7,)),
            pltpu.SemaphoreType.DMA((2,)),
            pltpu.SemaphoreType.DMA((2,)),
        ],
        compiler_params=pltpu.CompilerParams(
            collective_id=0, has_side_effects=True, vmem_limit_bytes=56 * 1024 * 1024
        ),
        cost_estimate=pl.CostEstimate(
            flops=3_400_000_000, bytes_accessed=4_000_000, transcendentals=300_000
        ),
    )(*args)


def solution(mesh):
    wide = P("ctx", "tp")
    in_specs = (wide,) * 6 + (P(None, None, "tp"), wide, wide)
    return jax.shard_map(
        on_device, mesh=mesh, in_specs=in_specs, out_specs=(wide,) * 5, check_vma=False
    )
```

```python
import functools
import math

import jax
import jax.numpy as jnp
from jax import lax
from jax.experimental import pallas as pl
from jax.experimental.pallas import tpu as pltpu
from jax.sharding import PartitionSpec as P

HEAD_DIM = 128
ROWS = 128
CHANNELS = 1024
PEERS = 32
NARROW = 32
GROUP = 16
HELD = 2
TPS = 8
SHORT = 7
RIM = 16
SUPER = 16
LONG = 4096
TOTAL = 4096 * 512
F32 = jnp.float32
BF16 = jnp.bfloat16
MESH = pl.DeviceIdType.MESH


STEPS = (8, 24, 7, 25, 9, 23, 6, 26, 10, 22, 5, 27, 11, 21, 4, 28)
STEPS += (12, 20, 3, 29, 13, 19, 2, 30, 14, 18, 1, 31, 15, 17, 16)
INPUTS = 9


def dot(a, b, contract):
    return lax.dot_general(a, b, (contract, ((), ())), preferred_element_type=F32)


def kernel(
    q_hbm,
    k_hbm,
    v_hbm,
    hq_hbm,
    hk_hbm,
    hv_hbm,
    taps_hbm,
    filt_hbm,
    up_hbm,
    att_ref,
    qg_ref,
    ext,
    raw_ref,
    factor_ref,
    q_ref,
    k_ref,
    v_ref,
    hq_ref,
    hk_ref,
    hv_ref,
    taps_ref,
    filt_ref,
    up_ref,
    load_sem,
    rim_out,
    rim_in,
    kv_in,
    short,
    send_h,
    recv_h,
    send_m,
    recv_m,
    send_g,
    recv_g,
    send_c,
    recv_c,
    send_d,
    recv_d,
    send_f,
    recv_f,
    send_n,
    recv_n,
    edge_out,
    edge_in,
    raw_rows,
    padded_m,
    padded_g,
    left_m,
    left_g,
    weight_c,
    weight_d,
    gram,
    rim_send_sem,
    rim_recv_sem,
    kv_send_sem,
    kv_recv_sem,
    out_sem,
    in_sem,
    edge_send_sem,
    edge_recv_sem,
):
    hbm = (q_hbm, k_hbm, v_hbm, hq_hbm, hk_hbm, hv_hbm, filt_hbm, up_hbm, taps_hbm)
    me = lax.axis_index("ctx")
    tp = lax.axis_index("tp")
    after = (me + 1) % PEERS
    before = (me + PEERS - 1) % PEERS

    barrier = pltpu.get_barrier_semaphore()

    held = (q_ref, k_ref, v_ref, hq_ref, hk_ref, hv_ref, filt_ref, up_ref, taps_ref)
    loads = [pltpu.make_async_copy(hbm[n], held[n], load_sem.at[n]) for n in range(INPUTS)]
    for n in (3, 4, 5, 6, 1, 2, 8, 7, 0):
        loads[n].start()

    for step in STEPS:
        pl.semaphore_signal(
            barrier, inc=1, device_id=((me + step) % PEERS, tp), device_id_type=MESH
        )
    for step in range(1, TPS):
        pl.semaphore_signal(
            barrier, inc=1, device_id=(me, (tp + step) % TPS), device_id_type=MESH
        )

    for n in (3, 4, 5):
        loads[n].wait()
    rim_out[0:RIM] = hq_ref[ROWS - RIM : ROWS]
    rim_out[RIM : 2 * RIM] = hk_ref[ROWS - RIM : ROWS]
    rim_out[2 * RIM : 3 * RIM] = hv_ref[ROWS - RIM : ROWS]
    for n in range(3):
        ext[n, RIM : RIM + ROWS] = held[3 + n][...].astype(F32)
    loads[6].wait()
    for p in range(PEERS):
        send_h[p] = filt_ref[HELD * p : HELD * p + HELD]
    loads[1].wait()
    loads[2].wait()
    pl.semaphore_wait(barrier, PEERS - 1 + TPS - 1)

    def to_next(src, dst, send_sem, recv_sem, target):
        return pltpu.make_async_remote_copy(
            src_ref=src,
            dst_ref=dst,
            send_sem=send_sem,
            recv_sem=recv_sem,
            device_id=(target, tp),
            device_id_type=MESH,
        )

    rim_copy = to_next(rim_out, rim_in, rim_send_sem, rim_recv_sem, after)
    rim_copy.start()

    def send_one(src, dst, which, peer):
        to_next(src.at[peer], dst.at[me], out_sem.at[which], in_sem.at[which], peer).start()

    def keep(src, dst):
        dst[pl.ds(me, 1)] = src[pl.ds(me, 1)]

    def scatter(src, dst, which):
        for step in STEPS:
            send_one(src, dst, which, (me + step) % PEERS)
        keep(src, dst)

    def settle(ref, sem):
        part = ref.at[pl.ds(0, PEERS - 1)]
        pltpu.make_async_copy(part, part, sem).wait()

    kv_copies = [
        to_next(src, kv_in.at[n], kv_send_sem.at[n], kv_recv_sem.at[n], after)
        for n, src in enumerate((k_ref, v_ref))
    ]
    for copy in kv_copies:
        copy.start()
    scatter(send_h, recv_h, 0)

    rim_copy.wait_recv()
    for n in range(3):
        leading = rim_in[n * RIM : (n + 1) * RIM].astype(F32)
        ext[n, 0:RIM] = jnp.where(me > 0, leading, 0.0)

    def short_conv(n, lanes):
        total = taps_ref[n, 0:1, lanes] * ext[n, RIM : RIM + ROWS, lanes]
        for s in range(1, SHORT):
            total += taps_ref[n, s : s + 1, lanes] * ext[n, RIM - s : RIM - s + ROWS, lanes]
        return total

    mine = me // 4

    def by_chunk(compute, src, dst, which):
        def chunk_at(step):
            return (mine + 4 + ((step + 1) // 2) * (1 - 2 * (step % 2))) % 8

        @pl.loop(0, 7)
        def _(step):
            chunk = chunk_at(step)
            compute(chunk)
            for n in range(4):
                send_one(src, dst, which, chunk * 4 + n)

        compute(mine)
        for n in range(1, 4):
            send_one(src, dst, which, mine * 4 + (me + n) % 4)
        keep(src, dst)

    def mixed_chunk(chunk):
        lanes = pl.ds(pl.multiple_of(chunk * 128, 128), 128)
        short_k = short_conv(1, lanes)
        short_v = short_conv(2, lanes)
        short[1, :, lanes] = short_k
        short[2, :, lanes] = short_v
        mixed = (short_k * short_v).T.astype(BF16)
        send_m[pl.ds(chunk * 4, 4)] = mixed.reshape(4, NARROW, ROWS)

    def delta_chunk(chunk):
        lanes = pl.ds(pl.multiple_of(chunk * 128, 128), 128)
        delta = (up_ref[:, lanes].astype(F32) * short_conv(0, lanes)).T.astype(BF16)
        send_g[pl.ds(chunk * 4, 4)] = delta.reshape(4, NARROW, ROWS)

    loads[8].wait()
    by_chunk(mixed_chunk, send_m, recv_m, 1)
    loads[7].wait()
    by_chunk(delta_chunk, send_g, recv_g, 2)

    row_at = lax.broadcasted_iota(jnp.int32, (ROWS, ROWS), 0)
    lane_at = lax.broadcasted_iota(jnp.int32, (ROWS, ROWS), 1)
    settle(recv_h, in_sem.at[0])
    for g in range(HELD):
        weight_c[g, 128:256, 0:128] = jnp.zeros((ROWS, ROWS), BF16)
        weight_d[g, 128:256, 0:128] = jnp.zeros((ROWS, ROWS), BF16)

    def turned(block, g):
        line = jnp.broadcast_to(recv_h[block, g : g + 1], (ROWS, ROWS))
        return pltpu.roll(line, 0, 1, stride=1, stride_axis=0)

    def build(d, last):
        top = pl.multiple_of(d * 256, 256)
        carried = []
        for g in range(HELD):
            even = turned(2 * d, g)
            odd = turned(2 * d + 1, g)
            tile_even = jnp.where(lane_at >= row_at, even, last[g]).astype(BF16)
            tile_odd = jnp.where(lane_at >= row_at, odd, even).astype(BF16)
            weight_c[g, pl.ds(top, 128), 0:128] = tile_even
            weight_c[g, pl.ds(top + 128, 128), 128:256] = tile_even
            weight_c[g, pl.ds(top, 128), 128:256] = tile_odd
            weight_c[g, pl.ds(top + 384, 128), 0:128] = tile_odd
            weight_d[g, 0:128, pl.ds(top, 128)] = tile_even
            weight_d[g, 128:256, pl.ds(top + 128, 128)] = tile_even
            weight_d[g, 0:128, pl.ds(top + 128, 128)] = tile_odd
            weight_d[g, 128:256, pl.ds(top + 256, 128)] = tile_odd
            carried.append(odd)
        return tuple(carried)

    lax.fori_loop(0, SUPER, build, (jnp.zeros((ROWS, ROWS), F32),) * HELD)

    half = SUPER * GROUP

    def paired(recv, g):
        rows = recv[:, g * GROUP : (g + 1) * GROUP, :].reshape(SUPER, 2, GROUP, ROWS)
        return rows[:, 0].reshape(half, ROWS), rows[:, 1].reshape(half, ROWS)

    def spread(send, result, g):
        both = jnp.stack(
            [
                result[:, 0:ROWS].reshape(SUPER, GROUP, ROWS),
                result[:, ROWS : 2 * ROWS].reshape(SUPER, GROUP, ROWS),
            ],
            axis=1,
        )
        send[:, g * GROUP : (g + 1) * GROUP, :] = both.reshape(PEERS, GROUP, ROWS)

    settle(recv_m, in_sem.at[1])
    padded_m[0:half] = jnp.zeros((half, 2 * ROWS), BF16)
    for g in range(HELD):
        even, odd = paired(recv_m, g)
        padded_m[half : 2 * half, 0:ROWS] = even
        padded_m[half : 2 * half, ROWS : 2 * ROWS] = odd
        for d in range(SUPER):
            left_m[:, d * 256 : (d + 1) * 256] = padded_m[half - GROUP * d : 2 * half - GROUP * d]
        conv = dot(left_m[...], weight_c[g, 0:LONG], ((1,), (0,))).astype(BF16)
        spread(send_c, conv, g)
    scatter(send_c, recv_c, 3)

    settle(recv_g, in_sem.at[2])
    padded_g[half : 2 * half] = jnp.zeros((half, 2 * ROWS), BF16)
    for g in range(HELD):
        even, odd = paired(recv_g, g)
        padded_g[0:half, 0:ROWS] = even
        padded_g[0:half, ROWS : 2 * ROWS] = odd
        for d in range(SUPER):
            left_g[g, :, d * 256 : (d + 1) * 256] = padded_g[GROUP * d : half + GROUP * d]
        back = dot(left_g[g], weight_d[g, :, 0:LONG], ((1,), (1,))).astype(BF16)
        spread(send_d, back, g)
    scatter(send_d, recv_d, 4)

    reversal = (row_at + lane_at == ROWS - 1).astype(BF16)
    upper = (lane_at < row_at) | (lane_at == ROWS - 1)
    for g in range(HELD):
        turned_m = jnp.concatenate(
            [dot(reversal, part, ((1,), (1,))).astype(BF16) for part in paired(recv_m, g)], 0
        )
        gram[:, 0:LONG] = dot(turned_m, left_g[g], ((1,), (0,)))
        gram[:, LONG : LONG + 2 * ROWS] = jnp.zeros((2 * ROWS, 2 * ROWS), F32)

        def slid(e):
            at = pl.multiple_of(e * ROWS, ROWS)
            tile = gram[0:ROWS, pl.ds(at, ROWS)] + gram[ROWS : 2 * ROWS, pl.ds(at + ROWS, ROWS)]
            return pltpu.roll(tile, 0, 1, stride=1, stride_axis=0)

        @pl.loop(0, PEERS // 4)
        def _(quad, slid=slid):
            tiles = [slid(quad * 4 + n) for n in range(5)]
            for n in range(4):
                merged = jnp.where(upper, tiles[n], tiles[n + 1])
                raw_rows[quad * 4 + n] = jnp.sum(merged.reshape(16, 8, ROWS), axis=0)

        raw = pltpu.roll(jnp.sum(raw_rows[...], axis=1), 1, 1)
        squares = jnp.sum(raw * raw, 0, keepdims=True)
        send_f[:, g : g + 1, :] = raw.reshape(PEERS, 1, ROWS)
        send_f[:, HELD + g : HELD + g + 1, :] = jnp.broadcast_to(
            squares.reshape(1, 1, ROWS), (PEERS, 1, ROWS)
        )
    scatter(send_f, recv_f, 5)

    for copy in kv_copies:
        copy.wait_recv()
    query_at = lax.broadcasted_iota(jnp.int32, (ROWS, 2 * ROWS), 0)
    key_at = lax.broadcasted_iota(jnp.int32, (ROWS, 2 * ROWS), 1) - ROWS
    first = jnp.where(me > 0, -ROWS, 0)
    allowed = (key_at <= query_at) & (key_at >= first)

    loads[0].wait()

    def attend(head):
        lanes = pl.ds(pl.multiple_of(head * HEAD_DIM, HEAD_DIM), HEAD_DIM)
        keys = jnp.concatenate([kv_in[0, :, lanes], k_ref[:, lanes]], 0)
        values = jnp.concatenate([kv_in[1, :, lanes], v_ref[:, lanes]], 0)
        scores = dot(q_ref[:, lanes], keys, ((1,), (1,))) * (1.0 / math.sqrt(HEAD_DIM))
        masked = jnp.where(allowed, scores, -jnp.inf)
        largest = jnp.max(masked, axis=1, keepdims=True)
        raised = jnp.exp(masked - largest)
        weights = (raised / jnp.sum(raised, axis=1, keepdims=True)).astype(BF16)
        att_ref[:, lanes] = dot(weights, values, ((1,), (0,))).astype(BF16)

    @pl.loop(0, CHANNELS // HEAD_DIM // 2)
    def _(pair):
        attend(2 * pair)
        attend(2 * pair + 1)

    def follow(n, source):
        def chunk_step(chunk, carry):
            lanes = pl.ds(pl.multiple_of(chunk * 128, 128), 128)
            part = source[pl.ds(chunk * 4, 4)].reshape(4 * NARROW, ROWS).astype(F32).T
            if n == 0:
                grads = ((0, up_ref[:, lanes].astype(F32) * part),)
            else:
                grads = ((1, part * short[2, :, lanes]), (2, part * short[1, :, lanes]))
            for which, grad in grads:
                ext[which, 0:ROWS, lanes] = grad
                edge_out[which, :, lanes] = grad[0:RIM].astype(BF16)
            return carry

        lax.fori_loop(0, CHANNELS // 128, chunk_step, 0)

    def edge_copy(n):
        part = pl.ds(0, 1) if n == 0 else pl.ds(1, 2)
        return to_next(
            edge_out.at[part],
            edge_in.at[part],
            edge_send_sem.at[n],
            edge_recv_sem.at[n],
            before,
        )

    def trail(n):
        trailing = edge_in[n].astype(F32)
        ext[n, ROWS : ROWS + RIM] = jnp.where(me < PEERS - 1, trailing, 0.0)

    settle(recv_c, in_sem.at[3])
    follow(0, recv_c)
    edge_copy(0).start()
    edge_copy(0).wait_recv()
    trail(0)

    @pl.loop(0, CHANNELS // 128)
    def _(chunk):
        lanes = pl.ds(pl.multiple_of(chunk * 128, 128), 128)
        qg_ref[:, lanes] = anti_short(ext, taps_ref, 0, lanes)

    settle(recv_d, in_sem.at[4])
    follow(1, recv_d)
    edge_copy(1).start()

    settle(recv_f, in_sem.at[5])
    squares = jnp.sum(recv_f[:, HELD : 2 * HELD, :], axis=0)
    squares = jnp.sum(squares, axis=0, keepdims=True)
    send_n[...] = jnp.broadcast_to(squares, (8, ROWS))

    def norm_copy(step):
        return pltpu.make_async_remote_copy(
            src_ref=send_n,
            dst_ref=recv_n.at[tp],
            send_sem=out_sem.at[6],
            recv_sem=in_sem.at[6],
            device_id=(me, (tp + step) % TPS),
            device_id_type=MESH,
        )

    @pl.loop(1, TPS)
    def _(step):
        norm_copy(step).start()

    recv_n[pl.ds(tp, 1)] = send_n[...].reshape(1, 8, ROWS)

    for p in range(PEERS):
        raw_ref[HELD * p : HELD * p + HELD] = recv_f[p, 0:HELD]
    edge_copy(1).wait_recv()
    trail(1)
    trail(2)

    part = recv_n.at[pl.ds(0, TPS - 1)]
    pltpu.make_async_copy(part, part, in_sem.at[6]).wait()
    total = jnp.sum(recv_n[:, 0, :], axis=0, keepdims=True)
    total = jnp.sum(total, axis=1, keepdims=True)
    factor = jnp.minimum(1.0, math.sqrt(TOTAL) / jnp.sqrt(total))
    factor_ref[...] = jnp.broadcast_to(factor, (8, ROWS))

    rim_copy.wait_send()
    for copy in kv_copies:
        copy.wait_send()
    for n in range(2):
        edge_copy(n).wait_send()
    for n, ref in enumerate((send_h, send_m, send_g, send_c, send_d, send_f)):
        settle(ref, out_sem.at[n])
    pltpu.make_async_copy(part, part, out_sem.at[6]).wait()


def anti_short(ext, taps_ref, n, lanes):
    total = taps_ref[n, 0:1, lanes] * ext[n, 0:ROWS, lanes]
    for s in range(1, SHORT):
        total += taps_ref[n, s : s + 1, lanes] * ext[n, s : s + ROWS, lanes]
    return total.astype(BF16)


def finish_kernel(
    ext, taps_ref, att, qg, raw_ref, factor_ref, att_hbm, qg_hbm, kg_hbm, vg_hbm, fg_hbm,
    fg_ref, grads, sems
):
    copies = [
        pltpu.make_async_copy(att, att_hbm, sems.at[0]),
        pltpu.make_async_copy(qg, qg_hbm, sems.at[1]),
        pltpu.make_async_copy(fg_ref, fg_hbm, sems.at[2]),
    ]
    copies[0].start()
    copies[1].start()
    fg_ref[...] = raw_ref[...] * factor_ref[0:1]
    copies[2].start()
    for n, out in enumerate((kg_hbm, vg_hbm)):
        for part in range(2):
            for step in range(4):
                lanes = slice(part * 512 + step * 128, part * 512 + step * 128 + 128)
                grads[n, :, lanes] = anti_short(ext, taps_ref, n + 1, lanes)
            lanes = slice(part * 512, part * 512 + 512)
            at = 3 + 2 * n + part
            copies.append(
                pltpu.make_async_copy(grads.at[n, :, lanes], out.at[:, lanes], sems.at[at])
            )
            copies[-1].start()
    for copy in copies:
        copy.wait()


def finish(ext, taps, att, qg, raw, factor):
    wide = jax.ShapeDtypeStruct((ROWS, CHANNELS), BF16)
    vmem = pl.BlockSpec(memory_space=pltpu.VMEM)
    return pl.pallas_call(
        finish_kernel,
        out_shape=(wide, wide, wide, wide, jax.ShapeDtypeStruct((64, ROWS), F32)),
        in_specs=[vmem] * 6,
        out_specs=(pl.BlockSpec(memory_space=pltpu.HBM),) * 5,
        scratch_shapes=[
            pltpu.VMEM((64, ROWS), F32),
            pltpu.VMEM((2, ROWS, CHANNELS), BF16),
            pltpu.SemaphoreType.DMA((7,)),
        ],
        compiler_params=pltpu.CompilerParams(vmem_limit_bytes=6 * 1024 * 1024),
    )(ext, taps, att, qg, raw, factor)


def on_device(*args):
    vmem = pl.BlockSpec(memory_space=pltpu.VMEM)
    anywhere = pl.BlockSpec(memory_space=pltpu.HBM)
    own = pltpu.VMEM((ROWS, CHANNELS), BF16)
    wide = jax.ShapeDtypeStruct((ROWS, CHANNELS), BF16)
    exchanged = pltpu.VMEM((PEERS, NARROW, ROWS), BF16)
    half = SUPER * GROUP
    args = list(args)
    taps = args[6]
    args[7] = args[7].T
    args = [pltpu.with_memory_space_constraint(arg, pltpu.HBM) for arg in args]
    att, qg, ext, raw, factor = pl.pallas_call(
        kernel,
        out_shape=(
            wide,
            wide,
            jax.ShapeDtypeStruct((3, ROWS + RIM, CHANNELS), F32),
            jax.ShapeDtypeStruct((64, ROWS), F32),
            jax.ShapeDtypeStruct((8, ROWS), F32),
        ),
        in_specs=[anywhere] * 9,
        out_specs=(vmem,) * 5,
        scratch_shapes=[
            *[own] * 6,
            pltpu.VMEM((3, SHORT, CHANNELS), F32),
            pltpu.VMEM((64, ROWS), F32),
            own,
            pltpu.SemaphoreType.DMA((INPUTS,)),
            pltpu.VMEM((3 * RIM, CHANNELS), BF16),
            pltpu.VMEM((3 * RIM, CHANNELS), BF16),
            pltpu.VMEM((2, ROWS, CHANNELS), BF16),
            pltpu.VMEM((3, ROWS, CHANNELS), F32),
            pltpu.VMEM((PEERS, HELD, ROWS), F32),
            pltpu.VMEM((PEERS, HELD, ROWS), F32),
            *[exchanged] * 8,
            pltpu.VMEM((PEERS, 2 * HELD, ROWS), F32),
            pltpu.VMEM((PEERS, 2 * HELD, ROWS), F32),
            pltpu.VMEM((8, ROWS), F32),
            pltpu.VMEM((TPS, 8, ROWS), F32),
            pltpu.VMEM((3, RIM, CHANNELS), BF16),
            pltpu.VMEM((3, RIM, CHANNELS), BF16),
            pltpu.VMEM((PEERS, 8, ROWS), F32),
            pltpu.VMEM((2 * half, 2 * ROWS), BF16),
            pltpu.VMEM((2 * half, 2 * ROWS), BF16),
            pltpu.VMEM((half, LONG), BF16),
            pltpu.VMEM((HELD, half, LONG), BF16),
            pltpu.VMEM((HELD, LONG + 256, 256), BF16),
            pltpu.VMEM((HELD, 256, LONG + 128), BF16),
            pltpu.VMEM((2 * ROWS, LONG + 2 * ROWS), F32),
            pltpu.SemaphoreType.DMA,
            pltpu.SemaphoreType.DMA,
            pltpu.SemaphoreType.DMA((2,)),
            pltpu.SemaphoreType.DMA((2,)),
            pltpu.SemaphoreType.DMA((7,)),
            pltpu.SemaphoreType.DMA((7,)),
            pltpu.SemaphoreType.DMA((2,)),
            pltpu.SemaphoreType.DMA((2,)),
        ],
        compiler_params=pltpu.CompilerParams(
            collective_id=0, has_side_effects=True, vmem_limit_bytes=32 * 1024 * 1024
        ),
        cost_estimate=pl.CostEstimate(
            flops=3_400_000_000, bytes_accessed=4_000_000, transcendentals=300_000
        ),
    )(*args)
    outs = finish(ext, taps, att, qg, raw, factor)
    return (*outs[:4], outs[4].T)


def solution(mesh):
    wide = P("ctx", "tp")
    in_specs = (wide,) * 6 + (P(None, None, "tp"), wide, wide)
    return jax.shard_map(
        on_device, mesh=mesh, in_specs=in_specs, out_specs=(wide,) * 5, check_vma=False
    )
```

```python
import functools
import math

import jax
import jax.numpy as jnp
from jax import lax
from jax.experimental import pallas as pl
from jax.experimental.pallas import tpu as pltpu
from jax.sharding import PartitionSpec as P

HEAD_DIM = 128
ROWS = 128
CHANNELS = 1024
PEERS = 32
NARROW = 32
GROUP = 16
HELD = 2
TPS = 8
SHORT = 7
RIM = 16
SUPER = 16
LONG = 4096
TOTAL = 4096 * 512
F32 = jnp.float32
BF16 = jnp.bfloat16
MESH = pl.DeviceIdType.MESH


STEPS = (8, 24, 7, 25, 9, 23, 6, 26, 10, 22, 5, 27, 11, 21, 4, 28)
STEPS += (12, 20, 3, 29, 13, 19, 2, 30, 14, 18, 1, 31, 15, 17, 16)
INPUTS = 9


def dot(a, b, contract):
    return lax.dot_general(a, b, (contract, ((), ())), preferred_element_type=F32)


def kernel(
    q_hbm,
    k_hbm,
    v_hbm,
    hq_hbm,
    hk_hbm,
    hv_hbm,
    taps_hbm,
    filt_hbm,
    up_hbm,
    att_ref,
    kg_ref,
    vg_ref,
    ext,
    raw_ref,
    factor_ref,
    q_ref,
    k_ref,
    v_ref,
    hq_ref,
    hk_ref,
    hv_ref,
    taps_ref,
    filt_ref,
    up_ref,
    load_sem,
    rim_out,
    rim_in,
    kv_in,
    short,
    send_h,
    recv_h,
    send_m,
    recv_m,
    send_g,
    recv_g,
    send_c,
    recv_c,
    send_d,
    recv_d,
    send_f,
    recv_f,
    send_n,
    recv_n,
    edge_out,
    edge_in,
    raw_rows,
    padded_m,
    padded_g,
    left_m,
    left_g,
    weight_c,
    weight_d,
    gram,
    rim_send_sem,
    rim_recv_sem,
    kv_send_sem,
    kv_recv_sem,
    out_sem,
    in_sem,
    edge_send_sem,
    edge_recv_sem,
):
    hbm = (q_hbm, k_hbm, v_hbm, hq_hbm, hk_hbm, hv_hbm, filt_hbm, up_hbm, taps_hbm)
    me = lax.axis_index("ctx")
    tp = lax.axis_index("tp")
    after = (me + 1) % PEERS
    before = (me + PEERS - 1) % PEERS

    barrier = pltpu.get_barrier_semaphore()

    held = (q_ref, k_ref, v_ref, hq_ref, hk_ref, hv_ref, filt_ref, up_ref, taps_ref)
    loads = [pltpu.make_async_copy(hbm[n], held[n], load_sem.at[n]) for n in range(INPUTS)]
    for n in (3, 4, 5, 1):
        loads[n].start()

    for step in STEPS[::-1]:
        pl.semaphore_signal(
            barrier, inc=1, device_id=((me + step) % PEERS, tp), device_id_type=MESH
        )
    for step in range(1, TPS):
        pl.semaphore_signal(
            barrier, inc=1, device_id=(me, (tp + step) % TPS), device_id_type=MESH
        )

    for n in (6, 8, 7, 2, 0):
        loads[n].start()
    for n in (3, 4, 5):
        loads[n].wait()
    rim_out[0:RIM] = hq_ref[ROWS - RIM : ROWS]
    rim_out[RIM : 2 * RIM] = hk_ref[ROWS - RIM : ROWS]
    rim_out[2 * RIM : 3 * RIM] = hv_ref[ROWS - RIM : ROWS]
    pl.semaphore_wait(barrier, PEERS - 1 + TPS - 1)

    def to_next(src, dst, send_sem, recv_sem, target):
        return pltpu.make_async_remote_copy(
            src_ref=src,
            dst_ref=dst,
            send_sem=send_sem,
            recv_sem=recv_sem,
            device_id=(target, tp),
            device_id_type=MESH,
        )

    rim_copy = to_next(rim_out, rim_in, rim_send_sem, rim_recv_sem, after)
    rim_copy.start()

    def send_one(src, dst, which, peer):
        to_next(src.at[peer], dst.at[me], out_sem.at[which], in_sem.at[which], peer).start()

    def keep(src, dst):
        dst[pl.ds(me, 1)] = src[pl.ds(me, 1)]

    def scatter(src, dst, which):
        for step in STEPS:
            send_one(src, dst, which, (me + step) % PEERS)
        keep(src, dst)

    def settle(ref, sem):
        part = ref.at[pl.ds(0, PEERS - 1)]
        pltpu.make_async_copy(part, part, sem).wait()

    loads[6].wait()
    for p in range(PEERS):
        send_h[p] = filt_ref[HELD * p : HELD * p + HELD]
    scatter(send_h, recv_h, 0)
    loads[1].wait()
    kv_copies = [
        to_next(src, kv_in.at[n], kv_send_sem.at[n], kv_recv_sem.at[n], after)
        for n, src in enumerate((k_ref, v_ref))
    ]
    kv_copies[0].start()

    for n in range(3):
        ext[n, RIM : RIM + ROWS] = held[3 + n][...].astype(F32)
        ext[n, 0:RIM] = jnp.zeros((RIM, CHANNELS), F32)
    loads[8].wait()

    def short_conv(n, rows, lanes):
        total = taps_ref[n, 0:1, lanes] * ext[n, RIM : RIM + rows, lanes]
        for s in range(1, SHORT):
            total += taps_ref[n, s : s + 1, lanes] * ext[n, RIM - s : RIM - s + rows, lanes]
        return total

    @pl.loop(0, CHANNELS // 128)
    def _(chunk):
        lanes = pl.ds(pl.multiple_of(chunk * 128, 128), 128)
        for n in range(3):
            short[n, :, lanes] = short_conv(n, ROWS, lanes)

    rim_copy.wait_recv()
    for n in range(3):
        leading = rim_in[n * RIM : (n + 1) * RIM].astype(F32)
        ext[n, 0:RIM] = jnp.where(me > 0, leading, 0.0)

    for n in range(3):
        short[n, 0:8] = short_conv(n, 8, slice(None))

    mine = me // 4

    def by_chunk(compute, src, dst, which):
        def chunk_at(step):
            return (mine + 4 + ((step + 1) // 2) * (1 - 2 * (step % 2))) % 8

        @pl.loop(0, 7)
        def _(step):
            chunk = chunk_at(step)
            compute(chunk)
            for n in range(4):
                send_one(src, dst, which, chunk * 4 + n)

        compute(mine)
        for n in range(1, 4):
            send_one(src, dst, which, mine * 4 + (me + n) % 4)
        keep(src, dst)

    def blocks_of(wide):
        return wide.T.astype(BF16).reshape(4, NARROW, ROWS)

    def delta_chunk(chunk):
        lanes = pl.ds(pl.multiple_of(chunk * 128, 128), 128)
        send_g[pl.ds(chunk * 4, 4)] = blocks_of(up_ref[:, lanes].astype(F32) * short[0, :, lanes])

    def mixed_chunk(chunk):
        lanes = pl.ds(pl.multiple_of(chunk * 128, 128), 128)
        send_m[pl.ds(chunk * 4, 4)] = blocks_of(short[1, :, lanes] * short[2, :, lanes])

    loads[7].wait()
    by_chunk(delta_chunk, send_g, recv_g, 2)
    loads[2].wait()
    by_chunk(mixed_chunk, send_m, recv_m, 1)

    kv_copies[1].start()
    row_at = lax.broadcasted_iota(jnp.int32, (ROWS, ROWS), 0)
    lane_at = lax.broadcasted_iota(jnp.int32, (ROWS, ROWS), 1)
    settle(recv_h, in_sem.at[0])
    for g in range(HELD):
        weight_c[g, 128:256, 0:128] = jnp.zeros((ROWS, ROWS), BF16)
        weight_d[g, 128:256, 0:128] = jnp.zeros((ROWS, ROWS), BF16)

    def turned(block, g):
        line = jnp.broadcast_to(recv_h[block, g : g + 1], (ROWS, ROWS))
        return pltpu.roll(line, 0, 1, stride=1, stride_axis=0)

    def build(d, last):
        top = pl.multiple_of(d * 256, 256)
        carried = []
        for g in range(HELD):
            even = turned(2 * d, g)
            odd = turned(2 * d + 1, g)
            tile_even = jnp.where(lane_at >= row_at, even, last[g]).astype(BF16)
            tile_odd = jnp.where(lane_at >= row_at, odd, even).astype(BF16)
            weight_c[g, pl.ds(top, 128), 0:128] = tile_even
            weight_c[g, pl.ds(top + 128, 128), 128:256] = tile_even
            weight_c[g, pl.ds(top, 128), 128:256] = tile_odd
            weight_c[g, pl.ds(top + 384, 128), 0:128] = tile_odd
            weight_d[g, 0:128, pl.ds(top, 128)] = tile_even
            weight_d[g, 128:256, pl.ds(top + 128, 128)] = tile_even
            weight_d[g, 0:128, pl.ds(top + 128, 128)] = tile_odd
            weight_d[g, 128:256, pl.ds(top + 256, 128)] = tile_odd
            carried.append(odd)
        return tuple(carried)

    lax.fori_loop(0, SUPER, build, (jnp.zeros((ROWS, ROWS), F32),) * HELD)

    half = SUPER * GROUP

    def paired(recv, g):
        rows = recv[:, g * GROUP : (g + 1) * GROUP, :].reshape(SUPER, 2, GROUP, ROWS)
        return rows[:, 0].reshape(half, ROWS), rows[:, 1].reshape(half, ROWS)

    def spread(send, result, g):
        both = jnp.stack(
            [
                result[:, 0:ROWS].reshape(SUPER, GROUP, ROWS),
                result[:, ROWS : 2 * ROWS].reshape(SUPER, GROUP, ROWS),
            ],
            axis=1,
        )
        send[:, g * GROUP : (g + 1) * GROUP, :] = both.reshape(PEERS, GROUP, ROWS)

    settle(recv_g, in_sem.at[2])
    padded_g[half : 2 * half] = jnp.zeros((half, 2 * ROWS), BF16)
    for g in range(HELD):
        even, odd = paired(recv_g, g)
        padded_g[0:half, 0:ROWS] = even
        padded_g[0:half, ROWS : 2 * ROWS] = odd
        for d in range(SUPER):
            left_g[g, :, d * 256 : (d + 1) * 256] = padded_g[GROUP * d : half + GROUP * d]
        back = dot(left_g[g], weight_d[g, :, 0:LONG], ((1,), (1,))).astype(BF16)
        spread(send_d, back, g)
    scatter(send_d, recv_d, 4)

    settle(recv_m, in_sem.at[1])
    padded_m[0:half] = jnp.zeros((half, 2 * ROWS), BF16)
    for g in range(HELD):
        even, odd = paired(recv_m, g)
        padded_m[half : 2 * half, 0:ROWS] = even
        padded_m[half : 2 * half, ROWS : 2 * ROWS] = odd
        for d in range(SUPER):
            left_m[:, d * 256 : (d + 1) * 256] = padded_m[half - GROUP * d : 2 * half - GROUP * d]
        conv = dot(left_m[...], weight_c[g, 0:LONG], ((1,), (0,))).astype(BF16)
        spread(send_c, conv, g)
    scatter(send_c, recv_c, 3)

    reversal = (row_at + lane_at == ROWS - 1).astype(BF16)
    upper = (lane_at < row_at) | (lane_at == ROWS - 1)
    for g in range(HELD):
        turned_m = jnp.concatenate(
            [dot(reversal, part, ((1,), (1,))).astype(BF16) for part in paired(recv_m, g)], 0
        )
        gram[:, 0:LONG] = dot(turned_m, left_g[g], ((1,), (0,)))
        gram[:, LONG : LONG + 2 * ROWS] = jnp.zeros((2 * ROWS, 2 * ROWS), F32)

        def slid(e):
            at = pl.multiple_of(e * ROWS, ROWS)
            tile = gram[0:ROWS, pl.ds(at, ROWS)] + gram[ROWS : 2 * ROWS, pl.ds(at + ROWS, ROWS)]
            return pltpu.roll(tile, 0, 1, stride=1, stride_axis=0)

        @pl.loop(0, PEERS // 4)
        def _(quad, slid=slid):
            tiles = [slid(quad * 4 + n) for n in range(5)]
            for n in range(4):
                merged = jnp.where(upper, tiles[n], tiles[n + 1])
                raw_rows[quad * 4 + n] = jnp.sum(merged.reshape(16, 8, ROWS), axis=0)

        raw = pltpu.roll(jnp.sum(raw_rows[...], axis=1), 1, 1)
        squares = jnp.sum(raw * raw, 0, keepdims=True)
        send_f[:, g : g + 1, :] = raw.reshape(PEERS, 1, ROWS)
        send_f[:, HELD + g : HELD + g + 1, :] = jnp.broadcast_to(
            squares.reshape(1, 1, ROWS), (PEERS, 1, ROWS)
        )
    scatter(send_f, recv_f, 5)

    for copy in kv_copies:
        copy.wait_recv()
    query_at = lax.broadcasted_iota(jnp.int32, (ROWS, 2 * ROWS), 0)
    key_at = lax.broadcasted_iota(jnp.int32, (ROWS, 2 * ROWS), 1) - ROWS
    first = jnp.where(me > 0, -ROWS, 0)
    allowed = (key_at <= query_at) & (key_at >= first)

    loads[0].wait()

    def attend(head):
        lanes = pl.ds(pl.multiple_of(head * HEAD_DIM, HEAD_DIM), HEAD_DIM)
        keys = jnp.concatenate([kv_in[0, :, lanes], k_ref[:, lanes]], 0)
        values = jnp.concatenate([kv_in[1, :, lanes], v_ref[:, lanes]], 0)
        scores = dot(q_ref[:, lanes], keys, ((1,), (1,))) * (1.0 / math.sqrt(HEAD_DIM))
        masked = jnp.where(allowed, scores, -jnp.inf)
        largest = jnp.max(masked, axis=1, keepdims=True)
        raised = jnp.exp(masked - largest)
        weights = (raised / jnp.sum(raised, axis=1, keepdims=True)).astype(BF16)
        att_ref[:, lanes] = dot(weights, values, ((1,), (0,))).astype(BF16)

    @pl.loop(0, CHANNELS // HEAD_DIM // 2)
    def _(pair):
        attend(2 * pair)
        attend(2 * pair + 1)

    def follow(n, source):
        def chunk_step(chunk, carry):
            lanes = pl.ds(pl.multiple_of(chunk * 128, 128), 128)
            part = source[pl.ds(chunk * 4, 4)].reshape(4 * NARROW, ROWS).astype(F32).T
            if n == 0:
                grads = ((0, up_ref[:, lanes].astype(F32) * part),)
            else:
                grads = ((1, part * short[2, :, lanes]), (2, part * short[1, :, lanes]))
            for which, grad in grads:
                ext[which, 0:ROWS, lanes] = grad
                edge_out[which, :, lanes] = grad[0:RIM].astype(BF16)
            return carry

        lax.fori_loop(0, CHANNELS // 128, chunk_step, 0)

    def edge_copy(n):
        part = pl.ds(0, 1) if n == 0 else pl.ds(1, 2)
        return to_next(
            edge_out.at[part],
            edge_in.at[part],
            edge_send_sem.at[n],
            edge_recv_sem.at[n],
            before,
        )

    def trail(n):
        trailing = edge_in[n].astype(F32)
        ext[n, ROWS : ROWS + RIM] = jnp.where(me < PEERS - 1, trailing, 0.0)

    settle(recv_d, in_sem.at[4])
    follow(1, recv_d)
    edge_copy(1).start()

    settle(recv_f, in_sem.at[5])
    squares = jnp.sum(recv_f[:, HELD : 2 * HELD, :], axis=0)
    squares = jnp.sum(squares, axis=0, keepdims=True)
    send_n[...] = jnp.broadcast_to(squares, (8, ROWS))

    def norm_copy(step):
        return pltpu.make_async_remote_copy(
            src_ref=send_n,
            dst_ref=recv_n.at[tp],
            send_sem=out_sem.at[6],
            recv_sem=in_sem.at[6],
            device_id=(me, (tp + step) % TPS),
            device_id_type=MESH,
        )

    for step in range(1, TPS):
        norm_copy(step).start()
    recv_n[pl.ds(tp, 1)] = send_n[...].reshape(1, 8, ROWS)
    for p in range(PEERS):
        raw_ref[HELD * p : HELD * p + HELD] = recv_f[p, 0:HELD]

    edge_copy(1).wait_recv()
    trail(1)
    trail(2)

    @pl.loop(0, CHANNELS // 128)
    def _(chunk):
        lanes = pl.ds(pl.multiple_of(chunk * 128, 128), 128)
        kg_ref[:, lanes] = anti_short(ext, taps_ref, 1, lanes)
        vg_ref[:, lanes] = anti_short(ext, taps_ref, 2, lanes)

    settle(recv_c, in_sem.at[3])
    follow(0, recv_c)
    edge_copy(0).start()
    part = recv_n.at[pl.ds(0, TPS - 1)]
    pltpu.make_async_copy(part, part, in_sem.at[6]).wait()
    total = jnp.sum(recv_n[:, 0, :], axis=0, keepdims=True)
    total = jnp.sum(total, axis=1, keepdims=True)
    factor = jnp.minimum(1.0, math.sqrt(TOTAL) / jnp.sqrt(total))
    factor_ref[...] = jnp.broadcast_to(factor, (8, ROWS))


    edge_copy(0).wait_recv()
    trail(0)

    rim_copy.wait_send()
    for copy in kv_copies:
        copy.wait_send()
    for n in range(2):
        edge_copy(n).wait_send()
    for n, ref in enumerate((send_h, send_m, send_g, send_c, send_d, send_f)):
        settle(ref, out_sem.at[n])
    pltpu.make_async_copy(part, part, out_sem.at[6]).wait()


def anti_short(ext, taps_ref, n, lanes):
    total = taps_ref[n, 0:1, lanes] * ext[n, 0:ROWS, lanes]
    for s in range(1, SHORT):
        total += taps_ref[n, s : s + 1, lanes] * ext[n, s : s + ROWS, lanes]
    return total.astype(BF16)


def finish_kernel(
    ext, taps_ref, att, kg, vg, raw_ref, factor_ref, att_hbm, qg_hbm, kg_hbm, vg_hbm, fg_hbm,
    fg_ref, grads, sems
):
    copies = [
        pltpu.make_async_copy(att, att_hbm, sems.at[0]),
        pltpu.make_async_copy(kg, kg_hbm, sems.at[1]),
        pltpu.make_async_copy(vg, vg_hbm, sems.at[2]),
        pltpu.make_async_copy(fg_ref, fg_hbm, sems.at[3]),
    ]
    for copy in copies[:3]:
        copy.start()
    fg_ref[...] = raw_ref[...] * factor_ref[0:1]
    copies[3].start()
    for part in range(4):
        for step in range(2):
            lanes = slice(part * 256 + step * 128, part * 256 + step * 128 + 128)
            grads[:, lanes] = anti_short(ext, taps_ref, 0, lanes)
        lanes = slice(part * 256, part * 256 + 256)
        copies.append(
            pltpu.make_async_copy(grads.at[:, lanes], qg_hbm.at[:, lanes], sems.at[4 + part])
        )
        copies[-1].start()
    for copy in copies:
        copy.wait()


def finish(*args):
    wide = jax.ShapeDtypeStruct((ROWS, CHANNELS), BF16)
    vmem = pl.BlockSpec(memory_space=pltpu.VMEM)
    return pl.pallas_call(
        finish_kernel,
        out_shape=(wide, wide, wide, wide, jax.ShapeDtypeStruct((64, ROWS), F32)),
        in_specs=[vmem] * 7,
        out_specs=(pl.BlockSpec(memory_space=pltpu.HBM),) * 5,
        scratch_shapes=[
            pltpu.VMEM((64, ROWS), F32),
            pltpu.VMEM((ROWS, CHANNELS), BF16),
            pltpu.SemaphoreType.DMA((8,)),
        ],
        compiler_params=pltpu.CompilerParams(vmem_limit_bytes=6 * 1024 * 1024),
    )(*args)


def on_device(*args):
    vmem = pl.BlockSpec(memory_space=pltpu.VMEM)
    anywhere = pl.BlockSpec(memory_space=pltpu.HBM)
    own = pltpu.VMEM((ROWS, CHANNELS), BF16)
    wide = jax.ShapeDtypeStruct((ROWS, CHANNELS), BF16)
    exchanged = pltpu.VMEM((PEERS, NARROW, ROWS), BF16)
    half = SUPER * GROUP
    args = list(args)
    taps = args[6]
    args[7] = args[7].T
    args = [pltpu.with_memory_space_constraint(arg, pltpu.HBM) for arg in args]
    att, kg, vg, ext, raw, factor = pl.pallas_call(
        kernel,
        out_shape=(
            wide,
            wide,
            wide,
            jax.ShapeDtypeStruct((3, ROWS + RIM, CHANNELS), F32),
            jax.ShapeDtypeStruct((64, ROWS), F32),
            jax.ShapeDtypeStruct((8, ROWS), F32),
        ),
        in_specs=[anywhere] * 9,
        out_specs=(vmem,) * 6,
        scratch_shapes=[
            *[own] * 6,
            pltpu.VMEM((3, SHORT, CHANNELS), F32),
            pltpu.VMEM((64, ROWS), F32),
            own,
            pltpu.SemaphoreType.DMA((INPUTS,)),
            pltpu.VMEM((3 * RIM, CHANNELS), BF16),
            pltpu.VMEM((3 * RIM, CHANNELS), BF16),
            pltpu.VMEM((2, ROWS, CHANNELS), BF16),
            pltpu.VMEM((3, ROWS, CHANNELS), F32),
            pltpu.VMEM((PEERS, HELD, ROWS), F32),
            pltpu.VMEM((PEERS, HELD, ROWS), F32),
            *[exchanged] * 8,
            pltpu.VMEM((PEERS, 2 * HELD, ROWS), F32),
            pltpu.VMEM((PEERS, 2 * HELD, ROWS), F32),
            pltpu.VMEM((8, ROWS), F32),
            pltpu.VMEM((TPS, 8, ROWS), F32),
            pltpu.VMEM((3, RIM, CHANNELS), BF16),
            pltpu.VMEM((3, RIM, CHANNELS), BF16),
            pltpu.VMEM((PEERS, 8, ROWS), F32),
            pltpu.VMEM((2 * half, 2 * ROWS), BF16),
            pltpu.VMEM((2 * half, 2 * ROWS), BF16),
            pltpu.VMEM((half, LONG), BF16),
            pltpu.VMEM((HELD, half, LONG), BF16),
            pltpu.VMEM((HELD, LONG + 256, 256), BF16),
            pltpu.VMEM((HELD, 256, LONG + 128), BF16),
            pltpu.VMEM((2 * ROWS, LONG + 2 * ROWS), F32),
            pltpu.SemaphoreType.DMA,
            pltpu.SemaphoreType.DMA,
            pltpu.SemaphoreType.DMA((2,)),
            pltpu.SemaphoreType.DMA((2,)),
            pltpu.SemaphoreType.DMA((7,)),
            pltpu.SemaphoreType.DMA((7,)),
            pltpu.SemaphoreType.DMA((2,)),
            pltpu.SemaphoreType.DMA((2,)),
        ],
        compiler_params=pltpu.CompilerParams(
            collective_id=0, has_side_effects=True, vmem_limit_bytes=32 * 1024 * 1024
        ),
        cost_estimate=pl.CostEstimate(
            flops=3_400_000_000, bytes_accessed=4_000_000, transcendentals=300_000
        ),
    )(*args)
    outs = finish(ext, taps, att, kg, vg, raw, factor)
    return (*outs[:4], outs[4].T)


def solution(mesh):
    wide = P("ctx", "tp")
    in_specs = (wide,) * 6 + (P(None, None, "tp"), wide, wide)
    return jax.shard_map(
        on_device, mesh=mesh, in_specs=in_specs, out_specs=(wide,) * 5, check_vma=False
    )
```

```python
import functools
import math

import jax
import jax.numpy as jnp
from jax import lax
from jax.experimental import pallas as pl
from jax.experimental.pallas import tpu as pltpu
from jax.sharding import PartitionSpec as P

HEAD_DIM = 128
ROWS = 128
CHANNELS = 1024
PEERS = 32
NARROW = 32
GROUP = 16
HELD = 2
TPS = 8
SHORT = 7
RIM = 16
SUPER = 16
LONG = 4096
TOTAL = 4096 * 512
F32 = jnp.float32
BF16 = jnp.bfloat16
MESH = pl.DeviceIdType.MESH


STEPS = (8, 24, 7, 25, 9, 23, 6, 26, 10, 22, 5, 27, 11, 21, 4, 28)
STEPS += (12, 20, 3, 29, 13, 19, 2, 30, 14, 18, 1, 31, 15, 17, 16)
INPUTS = 9


def dot(a, b, contract):
    return lax.dot_general(a, b, (contract, ((), ())), preferred_element_type=F32)


def kernel(
    q_hbm,
    k_hbm,
    v_hbm,
    hq_hbm,
    hk_hbm,
    hv_hbm,
    taps_hbm,
    filt_hbm,
    up_hbm,
    att_ref,
    kg_ref,
    vg_ref,
    ext,
    raw_ref,
    factor_ref,
    q_ref,
    k_ref,
    v_ref,
    hq_ref,
    hk_ref,
    hv_ref,
    taps_ref,
    filt_ref,
    up_ref,
    load_sem,
    rim_out,
    rim_in,
    kv_in,
    short,
    send_h,
    recv_h,
    send_m,
    recv_m,
    send_g,
    recv_g,
    send_c,
    recv_c,
    send_d,
    recv_d,
    send_f,
    recv_f,
    send_n,
    recv_n,
    edge_out,
    edge_in,
    raw_rows,
    padded_m,
    padded_g,
    left_m,
    left_g,
    weight_c,
    weight_d,
    gram,
    rim_send_sem,
    rim_recv_sem,
    kv_send_sem,
    kv_recv_sem,
    out_sem,
    in_sem,
    edge_send_sem,
    edge_recv_sem,
):
    hbm = (q_hbm, k_hbm, v_hbm, hq_hbm, hk_hbm, hv_hbm, filt_hbm, up_hbm, taps_hbm)
    me = lax.axis_index("ctx")
    tp = lax.axis_index("tp")
    after = (me + 1) % PEERS
    before = (me + PEERS - 1) % PEERS

    barrier = pltpu.get_barrier_semaphore()

    held = (q_ref, k_ref, v_ref, hq_ref, hk_ref, hv_ref, filt_ref, up_ref, taps_ref)
    loads = [pltpu.make_async_copy(hbm[n], held[n], load_sem.at[n]) for n in range(INPUTS)]
    for n in (3, 4, 5, 1):
        loads[n].start()

    for step in STEPS[::-1]:
        pl.semaphore_signal(
            barrier, inc=1, device_id=((me + step) % PEERS, tp), device_id_type=MESH
        )
    for step in range(1, TPS):
        pl.semaphore_signal(
            barrier, inc=1, device_id=(me, (tp + step) % TPS), device_id_type=MESH
        )

    for n in (6, 8, 7, 2, 0):
        loads[n].start()
    for n in (3, 4, 5):
        loads[n].wait()
    rim_out[0:RIM] = hq_ref[ROWS - RIM : ROWS]
    rim_out[RIM : 2 * RIM] = hk_ref[ROWS - RIM : ROWS]
    rim_out[2 * RIM : 3 * RIM] = hv_ref[ROWS - RIM : ROWS]
    pl.semaphore_wait(barrier, PEERS - 1 + TPS - 1)

    def to_next(src, dst, send_sem, recv_sem, target):
        return pltpu.make_async_remote_copy(
            src_ref=src,
            dst_ref=dst,
            send_sem=send_sem,
            recv_sem=recv_sem,
            device_id=(target, tp),
            device_id_type=MESH,
        )

    rim_copy = to_next(rim_out, rim_in, rim_send_sem, rim_recv_sem, after)
    rim_copy.start()

    def send_one(src, dst, which, peer):
        to_next(src.at[peer], dst.at[me], out_sem.at[which], in_sem.at[which], peer).start()

    def keep(src, dst):
        dst[pl.ds(me, 1)] = src[pl.ds(me, 1)]

    def scatter(src, dst, which):
        for step in STEPS:
            send_one(src, dst, which, (me + step) % PEERS)
        keep(src, dst)

    def settle(ref, sem):
        part = ref.at[pl.ds(0, PEERS - 1)]
        pltpu.make_async_copy(part, part, sem).wait()

    loads[6].wait()
    for p in range(PEERS):
        send_h[p] = filt_ref[HELD * p : HELD * p + HELD]
    scatter(send_h, recv_h, 0)
    loads[1].wait()
    kv_copies = [
        to_next(src, kv_in.at[n], kv_send_sem.at[n], kv_recv_sem.at[n], after)
        for n, src in enumerate((k_ref, v_ref))
    ]
    kv_copies[0].start()

    for n in range(3):
        ext[n, RIM : RIM + ROWS] = held[3 + n][...].astype(F32)
        ext[n, 0:RIM] = jnp.zeros((RIM, CHANNELS), F32)
    loads[8].wait()

    def short_conv(n, rows, lanes):
        total = taps_ref[n, 0:1, lanes] * ext[n, RIM : RIM + rows, lanes]
        for s in range(1, SHORT):
            total += taps_ref[n, s : s + 1, lanes] * ext[n, RIM - s : RIM - s + rows, lanes]
        return total

    @pl.loop(0, CHANNELS // 128)
    def _(chunk):
        lanes = pl.ds(pl.multiple_of(chunk * 128, 128), 128)
        for n in range(3):
            short[n, :, lanes] = short_conv(n, ROWS, lanes)

    rim_copy.wait_recv()
    for n in range(3):
        leading = rim_in[n * RIM : (n + 1) * RIM].astype(F32)
        ext[n, 0:RIM] = jnp.where(me > 0, leading, 0.0)

    for n in range(3):
        short[n, 0:8] = short_conv(n, 8, slice(None))

    mine = me // 4

    def by_chunk(compute, src, dst, which):
        def chunk_at(step):
            return (mine + 4 + ((step + 1) // 2) * (1 - 2 * (step % 2))) % 8

        @pl.loop(0, 7)
        def _(step):
            chunk = chunk_at(step)
            compute(chunk)
            for n in range(4):
                send_one(src, dst, which, chunk * 4 + n)

        compute(mine)
        for n in range(1, 4):
            send_one(src, dst, which, mine * 4 + (me + n) % 4)
        keep(src, dst)

    def blocks_of(wide):
        return wide.T.astype(BF16).reshape(4, NARROW, ROWS)

    def delta_chunk(chunk):
        lanes = pl.ds(pl.multiple_of(chunk * 128, 128), 128)
        send_g[pl.ds(chunk * 4, 4)] = blocks_of(up_ref[:, lanes].astype(F32) * short[0, :, lanes])

    def mixed_chunk(chunk):
        lanes = pl.ds(pl.multiple_of(chunk * 128, 128), 128)
        send_m[pl.ds(chunk * 4, 4)] = blocks_of(short[1, :, lanes] * short[2, :, lanes])

    loads[7].wait()
    by_chunk(delta_chunk, send_g, recv_g, 2)
    loads[2].wait()
    by_chunk(mixed_chunk, send_m, recv_m, 1)

    kv_copies[1].start()
    row_at = lax.broadcasted_iota(jnp.int32, (ROWS, ROWS), 0)
    lane_at = lax.broadcasted_iota(jnp.int32, (ROWS, ROWS), 1)
    settle(recv_h, in_sem.at[0])
    for g in range(HELD):
        weight_c[g, 128:256, 0:128] = jnp.zeros((ROWS, ROWS), BF16)
        weight_d[g, 128:256, 0:128] = jnp.zeros((ROWS, ROWS), BF16)

    def turned(block, g):
        line = jnp.broadcast_to(recv_h[block, g : g + 1], (ROWS, ROWS))
        return pltpu.roll(line, 0, 1, stride=1, stride_axis=0)

    def build(d, last):
        top = pl.multiple_of(d * 256, 256)
        carried = []
        for g in range(HELD):
            even = turned(2 * d, g)
            odd = turned(2 * d + 1, g)
            tile_even = jnp.where(lane_at >= row_at, even, last[g]).astype(BF16)
            tile_odd = jnp.where(lane_at >= row_at, odd, even).astype(BF16)
            weight_c[g, pl.ds(top, 128), 0:128] = tile_even
            weight_c[g, pl.ds(top + 128, 128), 128:256] = tile_even
            weight_c[g, pl.ds(top, 128), 128:256] = tile_odd
            weight_c[g, pl.ds(top + 384, 128), 0:128] = tile_odd
            weight_d[g, 0:128, pl.ds(top, 128)] = tile_even
            weight_d[g, 128:256, pl.ds(top + 128, 128)] = tile_even
            weight_d[g, 0:128, pl.ds(top + 128, 128)] = tile_odd
            weight_d[g, 128:256, pl.ds(top + 256, 128)] = tile_odd
            carried.append(odd)
        return tuple(carried)

    lax.fori_loop(0, SUPER, build, (jnp.zeros((ROWS, ROWS), F32),) * HELD)

    half = SUPER * GROUP

    def paired(recv, g):
        rows = recv[:, g * GROUP : (g + 1) * GROUP, :].reshape(SUPER, 2, GROUP, ROWS)
        return rows[:, 0].reshape(half, ROWS), rows[:, 1].reshape(half, ROWS)

    def spread(send, result, g):
        both = jnp.stack(
            [
                result[:, 0:ROWS].reshape(SUPER, GROUP, ROWS),
                result[:, ROWS : 2 * ROWS].reshape(SUPER, GROUP, ROWS),
            ],
            axis=1,
        )
        send[:, g * GROUP : (g + 1) * GROUP, :] = both.reshape(PEERS, GROUP, ROWS)

    settle(recv_g, in_sem.at[2])
    padded_g[half : 2 * half] = jnp.zeros((half, 2 * ROWS), BF16)
    for g in range(HELD):
        even, odd = paired(recv_g, g)
        padded_g[0:half, 0:ROWS] = even
        padded_g[0:half, ROWS : 2 * ROWS] = odd
        for d in range(SUPER):
            left_g[g, :, d * 256 : (d + 1) * 256] = padded_g[GROUP * d : half + GROUP * d]
        back = dot(left_g[g], weight_d[g, :, 0:LONG], ((1,), (1,))).astype(BF16)
        spread(send_d, back, g)
    scatter(send_d, recv_d, 4)

    settle(recv_m, in_sem.at[1])
    padded_m[0:half] = jnp.zeros((half, 2 * ROWS), BF16)
    for g in range(HELD):
        even, odd = paired(recv_m, g)
        padded_m[half : 2 * half, 0:ROWS] = even
        padded_m[half : 2 * half, ROWS : 2 * ROWS] = odd
        for d in range(SUPER):
            left_m[:, d * 256 : (d + 1) * 256] = padded_m[half - GROUP * d : 2 * half - GROUP * d]
        conv = dot(left_m[...], weight_c[g, 0:LONG], ((1,), (0,))).astype(BF16)
        spread(send_c, conv, g)
    scatter(send_c, recv_c, 3)

    reversal = (row_at + lane_at == ROWS - 1).astype(BF16)
    upper = (lane_at < row_at) | (lane_at == ROWS - 1)
    for g in range(HELD):
        turned_m = jnp.concatenate(
            [dot(reversal, part, ((1,), (1,))).astype(BF16) for part in paired(recv_m, g)], 0
        )
        gram[:, 0:LONG] = dot(turned_m, left_g[g], ((1,), (0,)))
        gram[:, LONG : LONG + 2 * ROWS] = jnp.zeros((2 * ROWS, 2 * ROWS), F32)

        def slid(e):
            at = pl.multiple_of(e * ROWS, ROWS)
            tile = gram[0:ROWS, pl.ds(at, ROWS)] + gram[ROWS : 2 * ROWS, pl.ds(at + ROWS, ROWS)]
            return pltpu.roll(tile, 0, 1, stride=1, stride_axis=0)

        @pl.loop(0, PEERS // 4)
        def _(quad, slid=slid):
            tiles = [slid(quad * 4 + n) for n in range(5)]
            for n in range(4):
                merged = jnp.where(upper, tiles[n], tiles[n + 1])
                raw_rows[quad * 4 + n] = jnp.sum(merged.reshape(16, 8, ROWS), axis=0)

        raw = pltpu.roll(jnp.sum(raw_rows[...], axis=1), 1, 1)
        squares = jnp.sum(raw * raw, 0, keepdims=True)
        send_f[:, g : g + 1, :] = raw.reshape(PEERS, 1, ROWS)
        send_f[:, HELD + g : HELD + g + 1, :] = jnp.broadcast_to(
            squares.reshape(1, 1, ROWS), (PEERS, 1, ROWS)
        )
    scatter(send_f, recv_f, 5)

    for copy in kv_copies:
        copy.wait_recv()
    query_at = lax.broadcasted_iota(jnp.int32, (ROWS, 2 * ROWS), 0)
    key_at = lax.broadcasted_iota(jnp.int32, (ROWS, 2 * ROWS), 1) - ROWS
    first = jnp.where(me > 0, -ROWS, 0)
    allowed = (key_at <= query_at) & (key_at >= first)

    loads[0].wait()

    def attend(head):
        lanes = pl.ds(pl.multiple_of(head * HEAD_DIM, HEAD_DIM), HEAD_DIM)
        keys = jnp.concatenate([kv_in[0, :, lanes], k_ref[:, lanes]], 0)
        values = jnp.concatenate([kv_in[1, :, lanes], v_ref[:, lanes]], 0)
        scores = dot(q_ref[:, lanes], keys, ((1,), (1,))) * (1.0 / math.sqrt(HEAD_DIM))
        masked = jnp.where(allowed, scores, -jnp.inf)
        largest = jnp.max(masked, axis=1, keepdims=True)
        raised = jnp.exp(masked - largest)
        weights = (raised / jnp.sum(raised, axis=1, keepdims=True)).astype(BF16)
        att_ref[:, lanes] = dot(weights, values, ((1,), (0,))).astype(BF16)

    @pl.loop(0, CHANNELS // HEAD_DIM // 2)
    def _(pair):
        attend(2 * pair)
        attend(2 * pair + 1)

    def follow(n, source):
        def chunk_step(chunk):
            lanes = pl.ds(pl.multiple_of(chunk * 128, 128), 128)
            part = source[pl.ds(chunk * 4, 4)].reshape(4 * NARROW, ROWS).astype(F32).T
            if n == 0:
                grads = ((0, up_ref[:, lanes].astype(F32) * part),)
            else:
                grads = ((1, part * short[2, :, lanes]), (2, part * short[1, :, lanes]))
            for which, grad in grads:
                ext[which, 0:ROWS, lanes] = grad
                edge_out[which, :, lanes] = grad[0:RIM].astype(BF16)

        @pl.loop(0, CHANNELS // 256)
        def _(pair):
            chunk_step(2 * pair)
            chunk_step(2 * pair + 1)

    def edge_copy(n):
        part = pl.ds(0, 1) if n == 0 else pl.ds(1, 2)
        return to_next(
            edge_out.at[part],
            edge_in.at[part],
            edge_send_sem.at[n],
            edge_recv_sem.at[n],
            before,
        )

    def trail(n):
        trailing = edge_in[n].astype(F32)
        ext[n, ROWS : ROWS + RIM] = jnp.where(me < PEERS - 1, trailing, 0.0)

    settle(recv_d, in_sem.at[4])
    follow(1, recv_d)
    edge_copy(1).start()

    settle(recv_f, in_sem.at[5])
    squares = jnp.sum(recv_f[:, HELD : 2 * HELD, :], axis=0)
    squares = jnp.sum(squares, axis=0, keepdims=True)
    send_n[...] = jnp.broadcast_to(squares, (8, ROWS))

    def norm_copy(step):
        return pltpu.make_async_remote_copy(
            src_ref=send_n,
            dst_ref=recv_n.at[tp],
            send_sem=out_sem.at[6],
            recv_sem=in_sem.at[6],
            device_id=(me, (tp + step) % TPS),
            device_id_type=MESH,
        )

    for step in range(1, TPS):
        norm_copy(step).start()
    recv_n[pl.ds(tp, 1)] = send_n[...].reshape(1, 8, ROWS)
    for p in range(PEERS):
        raw_ref[HELD * p : HELD * p + HELD] = recv_f[p, 0:HELD]

    settle(recv_c, in_sem.at[3])
    follow(0, recv_c)
    edge_copy(0).start()
    edge_copy(1).wait_recv()
    trail(1)
    trail(2)

    @pl.loop(0, CHANNELS // 128)
    def _(chunk):
        lanes = pl.ds(pl.multiple_of(chunk * 128, 128), 128)
        kg_ref[:, lanes] = anti_short(ext, taps_ref, 1, lanes)
        vg_ref[:, lanes] = anti_short(ext, taps_ref, 2, lanes)

    part = recv_n.at[pl.ds(0, TPS - 1)]
    pltpu.make_async_copy(part, part, in_sem.at[6]).wait()
    total = jnp.sum(recv_n[:, 0, :], axis=0, keepdims=True)
    total = jnp.sum(total, axis=1, keepdims=True)
    factor = jnp.minimum(1.0, math.sqrt(TOTAL) / jnp.sqrt(total))
    factor_ref[...] = jnp.broadcast_to(factor, (8, ROWS))


    edge_copy(0).wait_recv()
    trail(0)

    rim_copy.wait_send()
    for copy in kv_copies:
        copy.wait_send()
    for n in range(2):
        edge_copy(n).wait_send()
    for n, ref in enumerate((send_h, send_m, send_g, send_c, send_d, send_f)):
        settle(ref, out_sem.at[n])
    pltpu.make_async_copy(part, part, out_sem.at[6]).wait()


def anti_short(ext, taps_ref, n, lanes):
    total = taps_ref[n, 0:1, lanes] * ext[n, 0:ROWS, lanes]
    for s in range(1, SHORT):
        total += taps_ref[n, s : s + 1, lanes] * ext[n, s : s + ROWS, lanes]
    return total.astype(BF16)


def finish_kernel(
    ext, taps_ref, att, kg, vg, raw_ref, factor_ref, att_hbm, qg_hbm, kg_hbm, vg_hbm, fg_hbm,
    fg_ref, grads, sems
):
    copies = [
        pltpu.make_async_copy(att, att_hbm, sems.at[0]),
        pltpu.make_async_copy(kg, kg_hbm, sems.at[1]),
        pltpu.make_async_copy(vg, vg_hbm, sems.at[2]),
        pltpu.make_async_copy(fg_ref, fg_hbm, sems.at[3]),
    ]
    for copy in copies[:3]:
        copy.start()
    fg_ref[...] = raw_ref[...] * factor_ref[0:1]
    copies[3].start()
    for part in range(4):
        for step in range(2):
            lanes = slice(part * 256 + step * 128, part * 256 + step * 128 + 128)
            grads[:, lanes] = anti_short(ext, taps_ref, 0, lanes)
        lanes = slice(part * 256, part * 256 + 256)
        copies.append(
            pltpu.make_async_copy(grads.at[:, lanes], qg_hbm.at[:, lanes], sems.at[4 + part])
        )
        copies[-1].start()
    for copy in copies:
        copy.wait()


def finish(*args):
    wide = jax.ShapeDtypeStruct((ROWS, CHANNELS), BF16)
    vmem = pl.BlockSpec(memory_space=pltpu.VMEM)
    return pl.pallas_call(
        finish_kernel,
        out_shape=(wide, wide, wide, wide, jax.ShapeDtypeStruct((64, ROWS), F32)),
        in_specs=[vmem] * 7,
        out_specs=(pl.BlockSpec(memory_space=pltpu.HBM),) * 5,
        scratch_shapes=[
            pltpu.VMEM((64, ROWS), F32),
            pltpu.VMEM((ROWS, CHANNELS), BF16),
            pltpu.SemaphoreType.DMA((8,)),
        ],
        compiler_params=pltpu.CompilerParams(vmem_limit_bytes=6 * 1024 * 1024),
    )(*args)


def on_device(*args):
    vmem = pl.BlockSpec(memory_space=pltpu.VMEM)
    anywhere = pl.BlockSpec(memory_space=pltpu.HBM)
    own = pltpu.VMEM((ROWS, CHANNELS), BF16)
    wide = jax.ShapeDtypeStruct((ROWS, CHANNELS), BF16)
    exchanged = pltpu.VMEM((PEERS, NARROW, ROWS), BF16)
    half = SUPER * GROUP
    args = list(args)
    taps = args[6]
    args[7] = args[7].T
    args = [pltpu.with_memory_space_constraint(arg, pltpu.HBM) for arg in args]
    att, kg, vg, ext, raw, factor = pl.pallas_call(
        kernel,
        out_shape=(
            wide,
            wide,
            wide,
            jax.ShapeDtypeStruct((3, ROWS + RIM, CHANNELS), F32),
            jax.ShapeDtypeStruct((64, ROWS), F32),
            jax.ShapeDtypeStruct((8, ROWS), F32),
        ),
        in_specs=[anywhere] * 9,
        out_specs=(vmem,) * 6,
        scratch_shapes=[
            *[own] * 6,
            pltpu.VMEM((3, SHORT, CHANNELS), F32),
            pltpu.VMEM((64, ROWS), F32),
            own,
            pltpu.SemaphoreType.DMA((INPUTS,)),
            pltpu.VMEM((3 * RIM, CHANNELS), BF16),
            pltpu.VMEM((3 * RIM, CHANNELS), BF16),
            pltpu.VMEM((2, ROWS, CHANNELS), BF16),
            pltpu.VMEM((3, ROWS, CHANNELS), F32),
            pltpu.VMEM((PEERS, HELD, ROWS), F32),
            pltpu.VMEM((PEERS, HELD, ROWS), F32),
            *[exchanged] * 8,
            pltpu.VMEM((PEERS, 2 * HELD, ROWS), F32),
            pltpu.VMEM((PEERS, 2 * HELD, ROWS), F32),
            pltpu.VMEM((8, ROWS), F32),
            pltpu.VMEM((TPS, 8, ROWS), F32),
            pltpu.VMEM((3, RIM, CHANNELS), BF16),
            pltpu.VMEM((3, RIM, CHANNELS), BF16),
            pltpu.VMEM((PEERS, 8, ROWS), F32),
            pltpu.VMEM((2 * half, 2 * ROWS), BF16),
            pltpu.VMEM((2 * half, 2 * ROWS), BF16),
            pltpu.VMEM((half, LONG), BF16),
            pltpu.VMEM((HELD, half, LONG), BF16),
            pltpu.VMEM((HELD, LONG + 256, 256), BF16),
            pltpu.VMEM((HELD, 256, LONG + 128), BF16),
            pltpu.VMEM((2 * ROWS, LONG + 2 * ROWS), F32),
            pltpu.SemaphoreType.DMA,
            pltpu.SemaphoreType.DMA,
            pltpu.SemaphoreType.DMA((2,)),
            pltpu.SemaphoreType.DMA((2,)),
            pltpu.SemaphoreType.DMA((7,)),
            pltpu.SemaphoreType.DMA((7,)),
            pltpu.SemaphoreType.DMA((2,)),
            pltpu.SemaphoreType.DMA((2,)),
        ],
        compiler_params=pltpu.CompilerParams(
            collective_id=0, has_side_effects=True, vmem_limit_bytes=32 * 1024 * 1024
        ),
        cost_estimate=pl.CostEstimate(
            flops=3_400_000_000, bytes_accessed=4_000_000, transcendentals=300_000
        ),
    )(*args)
    outs = finish(ext, taps, att, kg, vg, raw, factor)
    return (*outs[:4], outs[4].T)


def solution(mesh):
    wide = P("ctx", "tp")
    in_specs = (wide,) * 6 + (P(None, None, "tp"), wide, wide)
    return jax.shard_map(
        on_device, mesh=mesh, in_specs=in_specs, out_specs=(wide,) * 5, check_vma=False
    )
```

```python
import functools
import math

import jax
import jax.numpy as jnp
from jax import lax
from jax.experimental import pallas as pl
from jax.experimental.pallas import tpu as pltpu
from jax.sharding import PartitionSpec as P

HEAD_DIM = 128
ROWS = 128
CHANNELS = 1024
PEERS = 32
NARROW = 32
GROUP = 16
HELD = 2
TPS = 8
SHORT = 7
RIM = 16
SUPER = 16
LONG = 4096
TOTAL = 4096 * 512
F32 = jnp.float32
BF16 = jnp.bfloat16
MESH = pl.DeviceIdType.MESH


STEPS = (8, 24, 7, 25, 9, 23, 6, 26, 10, 22, 5, 27, 11, 21, 4, 28)
STEPS += (12, 20, 3, 29, 13, 19, 2, 30, 14, 18, 1, 31, 15, 17, 16)
INPUTS = 9


def dot(a, b, contract):
    return lax.dot_general(a, b, (contract, ((), ())), preferred_element_type=F32)


def kernel(
    q_hbm,
    k_hbm,
    v_hbm,
    hq_hbm,
    hk_hbm,
    hv_hbm,
    taps_hbm,
    filt_hbm,
    up_hbm,
    att_ref,
    kg_ref,
    vg_ref,
    ext,
    raw_ref,
    factor_ref,
    q_ref,
    k_ref,
    v_ref,
    hq_ref,
    hk_ref,
    hv_ref,
    taps_ref,
    filt_ref,
    up_ref,
    load_sem,
    rim_out,
    rim_in,
    kv_in,
    short,
    send_h,
    recv_h,
    send_m,
    recv_m,
    send_g,
    recv_g,
    send_c,
    recv_c,
    send_d,
    recv_d,
    send_f,
    recv_f,
    send_n,
    recv_n,
    edge_out,
    edge_in,
    raw_rows,
    padded_m,
    padded_g,
    left_m,
    left_g,
    weight_c,
    weight_d,
    gram,
    rim_send_sem,
    rim_recv_sem,
    kv_send_sem,
    kv_recv_sem,
    out_sem,
    in_sem,
    edge_send_sem,
    edge_recv_sem,
):
    hbm = (q_hbm, k_hbm, v_hbm, hq_hbm, hk_hbm, hv_hbm, filt_hbm, up_hbm, taps_hbm)
    me = lax.axis_index("ctx")
    tp = lax.axis_index("tp")
    after = (me + 1) % PEERS
    before = (me + PEERS - 1) % PEERS

    barrier = pltpu.get_barrier_semaphore()

    held = (q_ref, k_ref, v_ref, hq_ref, hk_ref, hv_ref, filt_ref, up_ref, taps_ref)
    loads = [pltpu.make_async_copy(hbm[n], held[n], load_sem.at[n]) for n in range(INPUTS)]
    for step in STEPS[::-1]:
        pl.semaphore_signal(
            barrier, inc=1, device_id=((me + step) % PEERS, tp), device_id_type=MESH
        )
    for step in range(1, TPS):
        pl.semaphore_signal(
            barrier, inc=1, device_id=(me, (tp + step) % TPS), device_id_type=MESH
        )

    for n in (3, 4, 5, 1, 6, 8, 7, 2, 0):
        loads[n].start()
    for n in (3, 4, 5):
        loads[n].wait()
    rim_out[0:RIM] = hq_ref[ROWS - RIM : ROWS]
    rim_out[RIM : 2 * RIM] = hk_ref[ROWS - RIM : ROWS]
    rim_out[2 * RIM : 3 * RIM] = hv_ref[ROWS - RIM : ROWS]
    for n in range(3):
        ext[n, RIM : RIM + ROWS] = held[3 + n][...].astype(F32)
        ext[n, 0:RIM] = jnp.zeros((RIM, CHANNELS), F32)
    loads[8].wait()

    def short_conv(n, rows, lanes):
        total = taps_ref[n, 0:1, lanes] * ext[n, RIM : RIM + rows, lanes]
        for s in range(1, SHORT):
            total += taps_ref[n, s : s + 1, lanes] * ext[n, RIM - s : RIM - s + rows, lanes]
        return total

    @pl.loop(0, CHANNELS // 128)
    def _(chunk):
        lanes = pl.ds(pl.multiple_of(chunk * 128, 128), 128)
        short[0, :, lanes] = short_conv(0, ROWS, lanes)

    pl.semaphore_wait(barrier, PEERS - 1 + TPS - 1)

    def to_next(src, dst, send_sem, recv_sem, target):
        return pltpu.make_async_remote_copy(
            src_ref=src,
            dst_ref=dst,
            send_sem=send_sem,
            recv_sem=recv_sem,
            device_id=(target, tp),
            device_id_type=MESH,
        )

    rim_copy = to_next(rim_out, rim_in, rim_send_sem, rim_recv_sem, after)
    rim_copy.start()

    def send_one(src, dst, which, peer):
        to_next(src.at[peer], dst.at[me], out_sem.at[which], in_sem.at[which], peer).start()

    def keep(src, dst):
        dst[pl.ds(me, 1)] = src[pl.ds(me, 1)]

    def scatter(src, dst, which):
        for step in STEPS:
            send_one(src, dst, which, (me + step) % PEERS)
        keep(src, dst)

    def settle(ref, sem):
        part = ref.at[pl.ds(0, PEERS - 1)]
        pltpu.make_async_copy(part, part, sem).wait()

    loads[6].wait()
    for p in range(PEERS):
        send_h[p] = filt_ref[HELD * p : HELD * p + HELD]
    scatter(send_h, recv_h, 0)
    loads[1].wait()
    kv_copies = [
        to_next(src, kv_in.at[n], kv_send_sem.at[n], kv_recv_sem.at[n], after)
        for n, src in enumerate((k_ref, v_ref))
    ]
    kv_copies[0].start()

    rim_copy.wait_recv()
    for n in range(3):
        leading = rim_in[n * RIM : (n + 1) * RIM].astype(F32)
        ext[n, 0:RIM] = jnp.where(me > 0, leading, 0.0)

    short[0, 0:8] = short_conv(0, 8, slice(None))

    mine = me // 4

    def by_chunk(compute, src, dst, which):
        def chunk_at(step):
            return (mine + 4 + ((step + 1) // 2) * (1 - 2 * (step % 2))) % 8

        @pl.loop(0, 7)
        def _(step):
            chunk = chunk_at(step)
            compute(chunk)
            for n in range(4):
                send_one(src, dst, which, chunk * 4 + n)

        compute(mine)
        for n in range(1, 4):
            send_one(src, dst, which, mine * 4 + (me + n) % 4)
        keep(src, dst)

    def blocks_of(wide):
        return wide.T.astype(BF16).reshape(4, NARROW, ROWS)

    def delta_chunk(chunk):
        lanes = pl.ds(pl.multiple_of(chunk * 128, 128), 128)
        send_g[pl.ds(chunk * 4, 4)] = blocks_of(up_ref[:, lanes].astype(F32) * short[0, :, lanes])

    def mixed_chunk(chunk):
        lanes = pl.ds(pl.multiple_of(chunk * 128, 128), 128)
        for n in (1, 2):
            short[n, :, lanes] = short_conv(n, ROWS, lanes)
        send_m[pl.ds(chunk * 4, 4)] = blocks_of(short[1, :, lanes] * short[2, :, lanes])

    loads[7].wait()
    by_chunk(delta_chunk, send_g, recv_g, 2)
    loads[2].wait()
    by_chunk(mixed_chunk, send_m, recv_m, 1)

    kv_copies[1].start()
    row_at = lax.broadcasted_iota(jnp.int32, (ROWS, ROWS), 0)
    lane_at = lax.broadcasted_iota(jnp.int32, (ROWS, ROWS), 1)
    settle(recv_h, in_sem.at[0])
    for g in range(HELD):
        weight_c[g, 128:256, 0:128] = jnp.zeros((ROWS, ROWS), BF16)
        weight_d[g, 128:256, 0:128] = jnp.zeros((ROWS, ROWS), BF16)

    def turned(block, g):
        line = jnp.broadcast_to(recv_h[block, g : g + 1], (ROWS, ROWS))
        return pltpu.roll(line, 0, 1, stride=1, stride_axis=0)

    def build(d, last):
        top = pl.multiple_of(d * 256, 256)
        carried = []
        for g in range(HELD):
            even = turned(2 * d, g)
            odd = turned(2 * d + 1, g)
            tile_even = jnp.where(lane_at >= row_at, even, last[g]).astype(BF16)
            tile_odd = jnp.where(lane_at >= row_at, odd, even).astype(BF16)
            weight_c[g, pl.ds(top, 128), 0:128] = tile_even
            weight_c[g, pl.ds(top + 128, 128), 128:256] = tile_even
            weight_c[g, pl.ds(top, 128), 128:256] = tile_odd
            weight_c[g, pl.ds(top + 384, 128), 0:128] = tile_odd
            weight_d[g, 0:128, pl.ds(top, 128)] = tile_even
            weight_d[g, 128:256, pl.ds(top + 128, 128)] = tile_even
            weight_d[g, 0:128, pl.ds(top + 128, 128)] = tile_odd
            weight_d[g, 128:256, pl.ds(top + 256, 128)] = tile_odd
            carried.append(odd)
        return tuple(carried)

    lax.fori_loop(0, SUPER, build, (jnp.zeros((ROWS, ROWS), F32),) * HELD)

    half = SUPER * GROUP

    def paired(recv, g):
        rows = recv[:, g * GROUP : (g + 1) * GROUP, :].reshape(SUPER, 2, GROUP, ROWS)
        return rows[:, 0].reshape(half, ROWS), rows[:, 1].reshape(half, ROWS)

    def spread(send, result, g):
        both = jnp.stack(
            [
                result[:, 0:ROWS].reshape(SUPER, GROUP, ROWS),
                result[:, ROWS : 2 * ROWS].reshape(SUPER, GROUP, ROWS),
            ],
            axis=1,
        )
        send[:, g * GROUP : (g + 1) * GROUP, :] = both.reshape(PEERS, GROUP, ROWS)

    settle(recv_g, in_sem.at[2])
    padded_g[half : 2 * half] = jnp.zeros((half, 2 * ROWS), BF16)
    for g in range(HELD):
        even, odd = paired(recv_g, g)
        padded_g[0:half, 0:ROWS] = even
        padded_g[0:half, ROWS : 2 * ROWS] = odd
        for d in range(SUPER):
            left_g[g, :, d * 256 : (d + 1) * 256] = padded_g[GROUP * d : half + GROUP * d]
        back = dot(left_g[g], weight_d[g, :, 0:LONG], ((1,), (1,))).astype(BF16)
        spread(send_d, back, g)
    scatter(send_d, recv_d, 4)

    settle(recv_m, in_sem.at[1])
    padded_m[0:half] = jnp.zeros((half, 2 * ROWS), BF16)
    for g in range(HELD):
        even, odd = paired(recv_m, g)
        padded_m[half : 2 * half, 0:ROWS] = even
        padded_m[half : 2 * half, ROWS : 2 * ROWS] = odd
        for d in range(SUPER):
            left_m[:, d * 256 : (d + 1) * 256] = padded_m[half - GROUP * d : 2 * half - GROUP * d]
        conv = dot(left_m[...], weight_c[g, 0:LONG], ((1,), (0,))).astype(BF16)
        spread(send_c, conv, g)
    scatter(send_c, recv_c, 3)

    reversal = (row_at + lane_at == ROWS - 1).astype(BF16)
    upper = (lane_at < row_at) | (lane_at == ROWS - 1)
    for g in range(HELD):
        turned_m = jnp.concatenate(
            [dot(reversal, part, ((1,), (1,))).astype(BF16) for part in paired(recv_m, g)], 0
        )
        gram[:, 0:LONG] = dot(turned_m, left_g[g], ((1,), (0,)))
        gram[:, LONG : LONG + 2 * ROWS] = jnp.zeros((2 * ROWS, 2 * ROWS), F32)

        def slid(e):
            at = pl.multiple_of(e * ROWS, ROWS)
            tile = gram[0:ROWS, pl.ds(at, ROWS)] + gram[ROWS : 2 * ROWS, pl.ds(at + ROWS, ROWS)]
            return pltpu.roll(tile, 0, 1, stride=1, stride_axis=0)

        @pl.loop(0, PEERS // 4)
        def _(quad, slid=slid):
            tiles = [slid(quad * 4 + n) for n in range(5)]
            for n in range(4):
                merged = jnp.where(upper, tiles[n], tiles[n + 1])
                raw_rows[quad * 4 + n] = jnp.sum(merged.reshape(16, 8, ROWS), axis=0)

        raw = pltpu.roll(jnp.sum(raw_rows[...], axis=1), 1, 1)
        squares = jnp.sum(raw * raw, 0, keepdims=True)
        send_f[:, g : g + 1, :] = raw.reshape(PEERS, 1, ROWS)
        send_f[:, HELD + g : HELD + g + 1, :] = jnp.broadcast_to(
            squares.reshape(1, 1, ROWS), (PEERS, 1, ROWS)
        )
    scatter(send_f, recv_f, 5)

    for copy in kv_copies:
        copy.wait_recv()
    query_at = lax.broadcasted_iota(jnp.int32, (ROWS, 2 * ROWS), 0)
    key_at = lax.broadcasted_iota(jnp.int32, (ROWS, 2 * ROWS), 1) - ROWS
    first = jnp.where(me > 0, -ROWS, 0)
    allowed = (key_at <= query_at) & (key_at >= first)

    loads[0].wait()

    def attend(head):
        lanes = pl.ds(pl.multiple_of(head * HEAD_DIM, HEAD_DIM), HEAD_DIM)
        keys = jnp.concatenate([kv_in[0, :, lanes], k_ref[:, lanes]], 0)
        values = jnp.concatenate([kv_in[1, :, lanes], v_ref[:, lanes]], 0)
        scores = dot(q_ref[:, lanes], keys, ((1,), (1,))) * (1.0 / math.sqrt(HEAD_DIM))
        masked = jnp.where(allowed, scores, -jnp.inf)
        largest = jnp.max(masked, axis=1, keepdims=True)
        raised = jnp.exp(masked - largest)
        weights = (raised / jnp.sum(raised, axis=1, keepdims=True)).astype(BF16)
        att_ref[:, lanes] = dot(weights, values, ((1,), (0,))).astype(BF16)

    @pl.loop(0, CHANNELS // HEAD_DIM // 2)
    def _(pair):
        attend(2 * pair)
        attend(2 * pair + 1)

    def follow(n, source):
        def chunk_step(chunk):
            lanes = pl.ds(pl.multiple_of(chunk * 128, 128), 128)
            part = source[pl.ds(chunk * 4, 4)].reshape(4 * NARROW, ROWS).astype(F32).T
            if n == 0:
                grads = ((0, up_ref[:, lanes].astype(F32) * part),)
            else:
                grads = ((1, part * short[2, :, lanes]), (2, part * short[1, :, lanes]))
            for which, grad in grads:
                ext[which, 0:ROWS, lanes] = grad
                edge_out[which, :, lanes] = grad[0:RIM].astype(BF16)

        @pl.loop(0, CHANNELS // 256)
        def _(pair):
            chunk_step(2 * pair)
            chunk_step(2 * pair + 1)

    def edge_copy(n):
        part = pl.ds(0, 1) if n == 0 else pl.ds(1, 2)
        return to_next(
            edge_out.at[part],
            edge_in.at[part],
            edge_send_sem.at[n],
            edge_recv_sem.at[n],
            before,
        )

    def trail(n):
        trailing = edge_in[n].astype(F32)
        ext[n, ROWS : ROWS + RIM] = jnp.where(me < PEERS - 1, trailing, 0.0)

    settle(recv_d, in_sem.at[4])
    follow(1, recv_d)
    edge_copy(1).start()

    settle(recv_f, in_sem.at[5])
    squares = jnp.sum(recv_f[:, HELD : 2 * HELD, :], axis=0)
    squares = jnp.sum(squares, axis=0, keepdims=True)
    send_n[...] = jnp.broadcast_to(squares, (8, ROWS))

    def norm_copy(step):
        return pltpu.make_async_remote_copy(
            src_ref=send_n,
            dst_ref=recv_n.at[tp],
            send_sem=out_sem.at[6],
            recv_sem=in_sem.at[6],
            device_id=(me, (tp + step) % TPS),
            device_id_type=MESH,
        )

    for step in range(1, TPS):
        norm_copy(step).start()
    recv_n[pl.ds(tp, 1)] = send_n[...].reshape(1, 8, ROWS)
    for p in range(PEERS):
        raw_ref[HELD * p : HELD * p + HELD] = recv_f[p, 0:HELD]

    settle(recv_c, in_sem.at[3])
    follow(0, recv_c)
    edge_copy(0).start()
    edge_copy(1).wait_recv()
    trail(1)
    trail(2)

    @pl.loop(0, CHANNELS // 128)
    def _(chunk):
        lanes = pl.ds(pl.multiple_of(chunk * 128, 128), 128)
        kg_ref[:, lanes] = anti_short(ext, taps_ref, 1, lanes)
        vg_ref[:, lanes] = anti_short(ext, taps_ref, 2, lanes)

    part = recv_n.at[pl.ds(0, TPS - 1)]
    pltpu.make_async_copy(part, part, in_sem.at[6]).wait()
    total = jnp.sum(recv_n[:, 0, :], axis=0, keepdims=True)
    total = jnp.sum(total, axis=1, keepdims=True)
    factor = jnp.minimum(1.0, math.sqrt(TOTAL) / jnp.sqrt(total))
    factor_ref[...] = jnp.broadcast_to(factor, (8, ROWS))


    edge_copy(0).wait_recv()
    trail(0)

    rim_copy.wait_send()
    for copy in kv_copies:
        copy.wait_send()
    for n in range(2):
        edge_copy(n).wait_send()
    for n, ref in enumerate((send_h, send_m, send_g, send_c, send_d, send_f)):
        settle(ref, out_sem.at[n])
    pltpu.make_async_copy(part, part, out_sem.at[6]).wait()


def anti_short(ext, taps_ref, n, lanes):
    total = taps_ref[n, 0:1, lanes] * ext[n, 0:ROWS, lanes]
    for s in range(1, SHORT):
        total += taps_ref[n, s : s + 1, lanes] * ext[n, s : s + ROWS, lanes]
    return total.astype(BF16)


def finish_kernel(
    ext, taps_ref, att, kg, vg, raw_ref, factor_ref, att_hbm, qg_hbm, kg_hbm, vg_hbm, fg_hbm,
    fg_ref, grads, sems
):
    copies = [
        pltpu.make_async_copy(att, att_hbm, sems.at[0]),
        pltpu.make_async_copy(kg, kg_hbm, sems.at[1]),
        pltpu.make_async_copy(vg, vg_hbm, sems.at[2]),
        pltpu.make_async_copy(fg_ref, fg_hbm, sems.at[3]),
    ]
    for copy in copies[:3]:
        copy.start()
    fg_ref[...] = raw_ref[...] * factor_ref[0:1]
    copies[3].start()
    for part in range(4):
        for step in range(2):
            lanes = slice(part * 256 + step * 128, part * 256 + step * 128 + 128)
            grads[:, lanes] = anti_short(ext, taps_ref, 0, lanes)
        lanes = slice(part * 256, part * 256 + 256)
        copies.append(
            pltpu.make_async_copy(grads.at[:, lanes], qg_hbm.at[:, lanes], sems.at[4 + part])
        )
        copies[-1].start()
    for copy in copies:
        copy.wait()


def finish(*args):
    wide = jax.ShapeDtypeStruct((ROWS, CHANNELS), BF16)
    vmem = pl.BlockSpec(memory_space=pltpu.VMEM)
    return pl.pallas_call(
        finish_kernel,
        out_shape=(wide, wide, wide, wide, jax.ShapeDtypeStruct((64, ROWS), F32)),
        in_specs=[vmem] * 7,
        out_specs=(pl.BlockSpec(memory_space=pltpu.HBM),) * 5,
        scratch_shapes=[
            pltpu.VMEM((64, ROWS), F32),
            pltpu.VMEM((ROWS, CHANNELS), BF16),
            pltpu.SemaphoreType.DMA((8,)),
        ],
        compiler_params=pltpu.CompilerParams(vmem_limit_bytes=6 * 1024 * 1024),
    )(*args)


def on_device(*args):
    vmem = pl.BlockSpec(memory_space=pltpu.VMEM)
    anywhere = pl.BlockSpec(memory_space=pltpu.HBM)
    own = pltpu.VMEM((ROWS, CHANNELS), BF16)
    wide = jax.ShapeDtypeStruct((ROWS, CHANNELS), BF16)
    exchanged = pltpu.VMEM((PEERS, NARROW, ROWS), BF16)
    half = SUPER * GROUP
    args = list(args)
    taps = args[6]
    args[7] = args[7].T
    args = [pltpu.with_memory_space_constraint(arg, pltpu.HBM) for arg in args]
    att, kg, vg, ext, raw, factor = pl.pallas_call(
        kernel,
        out_shape=(
            wide,
            wide,
            wide,
            jax.ShapeDtypeStruct((3, ROWS + RIM, CHANNELS), F32),
            jax.ShapeDtypeStruct((64, ROWS), F32),
            jax.ShapeDtypeStruct((8, ROWS), F32),
        ),
        in_specs=[anywhere] * 9,
        out_specs=(vmem,) * 6,
        scratch_shapes=[
            *[own] * 6,
            pltpu.VMEM((3, SHORT, CHANNELS), F32),
            pltpu.VMEM((64, ROWS), F32),
            own,
            pltpu.SemaphoreType.DMA((INPUTS,)),
            pltpu.VMEM((3 * RIM, CHANNELS), BF16),
            pltpu.VMEM((3 * RIM, CHANNELS), BF16),
            pltpu.VMEM((2, ROWS, CHANNELS), BF16),
            pltpu.VMEM((3, ROWS, CHANNELS), F32),
            pltpu.VMEM((PEERS, HELD, ROWS), F32),
            pltpu.VMEM((PEERS, HELD, ROWS), F32),
            *[exchanged] * 8,
            pltpu.VMEM((PEERS, 2 * HELD, ROWS), F32),
            pltpu.VMEM((PEERS, 2 * HELD, ROWS), F32),
            pltpu.VMEM((8, ROWS), F32),
            pltpu.VMEM((TPS, 8, ROWS), F32),
            pltpu.VMEM((3, RIM, CHANNELS), BF16),
            pltpu.VMEM((3, RIM, CHANNELS), BF16),
            pltpu.VMEM((PEERS, 8, ROWS), F32),
            pltpu.VMEM((2 * half, 2 * ROWS), BF16),
            pltpu.VMEM((2 * half, 2 * ROWS), BF16),
            pltpu.VMEM((half, LONG), BF16),
            pltpu.VMEM((HELD, half, LONG), BF16),
            pltpu.VMEM((HELD, LONG + 256, 256), BF16),
            pltpu.VMEM((HELD, 256, LONG + 128), BF16),
            pltpu.VMEM((2 * ROWS, LONG + 2 * ROWS), F32),
            pltpu.SemaphoreType.DMA,
            pltpu.SemaphoreType.DMA,
            pltpu.SemaphoreType.DMA((2,)),
            pltpu.SemaphoreType.DMA((2,)),
            pltpu.SemaphoreType.DMA((7,)),
            pltpu.SemaphoreType.DMA((7,)),
            pltpu.SemaphoreType.DMA((2,)),
            pltpu.SemaphoreType.DMA((2,)),
        ],
        compiler_params=pltpu.CompilerParams(
            collective_id=0, has_side_effects=True, vmem_limit_bytes=32 * 1024 * 1024
        ),
        cost_estimate=pl.CostEstimate(
            flops=3_400_000_000, bytes_accessed=4_000_000, transcendentals=300_000
        ),
    )(*args)
    outs = finish(ext, taps, att, kg, vg, raw, factor)
    return (*outs[:4], outs[4].T)


def solution(mesh):
    wide = P("ctx", "tp")
    in_specs = (wide,) * 6 + (P(None, None, "tp"), wide, wide)
    return jax.shard_map(
        on_device, mesh=mesh, in_specs=in_specs, out_specs=(wide,) * 5, check_vma=False
    )
```

```python
import functools
import math

import jax
import jax.numpy as jnp
from jax import lax
from jax.experimental import pallas as pl
from jax.experimental.pallas import tpu as pltpu
from jax.sharding import PartitionSpec as P

HEAD_DIM = 128
ROWS = 128
CHANNELS = 1024
PEERS = 32
NARROW = 32
GROUP = 16
HELD = 2
TPS = 8
SHORT = 7
RIM = 16
SUPER = 16
LONG = 4096
TOTAL = 4096 * 512
F32 = jnp.float32
BF16 = jnp.bfloat16
MESH = pl.DeviceIdType.MESH


STEPS = (8, 24, 7, 25, 9, 23, 6, 26, 10, 22, 5, 27, 11, 21, 4, 28)
STEPS += (12, 20, 3, 29, 13, 19, 2, 30, 14, 18, 1, 31, 15, 17, 16)
INPUTS = 9


def dot(a, b, contract):
    return lax.dot_general(a, b, (contract, ((), ())), preferred_element_type=F32)


def kernel(
    q_hbm,
    k_hbm,
    v_hbm,
    hq_hbm,
    hk_hbm,
    hv_hbm,
    taps_hbm,
    filt_hbm,
    up_hbm,
    att_ref,
    kg_ref,
    vg_ref,
    ext,
    raw_ref,
    factor_ref,
    q_ref,
    k_ref,
    v_ref,
    hq_ref,
    hk_ref,
    hv_ref,
    taps_ref,
    filt_ref,
    up_ref,
    load_sem,
    rim_out,
    rim_in,
    kv_in,
    short,
    send_h,
    recv_h,
    send_m,
    recv_m,
    send_g,
    recv_g,
    send_c,
    recv_c,
    send_d,
    recv_d,
    send_f,
    recv_f,
    send_n,
    recv_n,
    edge_out,
    edge_in,
    raw_rows,
    padded_m,
    padded_g,
    left_m,
    left_g,
    weight_c,
    weight_d,
    gram,
    rim_send_sem,
    rim_recv_sem,
    kv_send_sem,
    kv_recv_sem,
    out_sem,
    in_sem,
    edge_send_sem,
    edge_recv_sem,
):
    hbm = (q_hbm, k_hbm, v_hbm, hq_hbm, hk_hbm, hv_hbm, filt_hbm, up_hbm, taps_hbm)
    me = lax.axis_index("ctx")
    tp = lax.axis_index("tp")
    after = (me + 1) % PEERS
    before = (me + PEERS - 1) % PEERS

    barrier = pltpu.get_barrier_semaphore()

    held = (q_ref, k_ref, v_ref, hq_ref, hk_ref, hv_ref, filt_ref, up_ref, taps_ref)
    loads = [pltpu.make_async_copy(hbm[n], held[n], load_sem.at[n]) for n in range(INPUTS)]
    for step in STEPS[::-1]:
        pl.semaphore_signal(
            barrier, inc=1, device_id=((me + step) % PEERS, tp), device_id_type=MESH
        )
    for step in range(1, TPS):
        pl.semaphore_signal(
            barrier, inc=1, device_id=(me, (tp + step) % TPS), device_id_type=MESH
        )

    for n in (3, 4, 5, 1, 6, 8, 7, 2, 0):
        loads[n].start()
    for n in (3, 4, 5):
        loads[n].wait()
    rim_out[0:RIM] = hq_ref[ROWS - RIM : ROWS]
    rim_out[RIM : 2 * RIM] = hk_ref[ROWS - RIM : ROWS]
    rim_out[2 * RIM : 3 * RIM] = hv_ref[ROWS - RIM : ROWS]
    for n in range(3):
        ext[n, RIM : RIM + ROWS] = held[3 + n][...].astype(F32)
        ext[n, 0:RIM] = jnp.zeros((RIM, CHANNELS), F32)
    loads[8].wait()

    def short_conv(n, rows, lanes):
        total = taps_ref[n, 0:1, lanes] * ext[n, RIM : RIM + rows, lanes]
        for s in range(1, SHORT):
            total += taps_ref[n, s : s + 1, lanes] * ext[n, RIM - s : RIM - s + rows, lanes]
        return total

    @pl.loop(0, CHANNELS // 128)
    def _(chunk):
        lanes = pl.ds(pl.multiple_of(chunk * 128, 128), 128)
        short[0, :, lanes] = short_conv(0, ROWS, lanes)

    pl.semaphore_wait(barrier, PEERS - 1 + TPS - 1)

    def to_next(src, dst, send_sem, recv_sem, target):
        return pltpu.make_async_remote_copy(
            src_ref=src,
            dst_ref=dst,
            send_sem=send_sem,
            recv_sem=recv_sem,
            device_id=(target, tp),
            device_id_type=MESH,
        )

    rim_copy = to_next(rim_out, rim_in, rim_send_sem, rim_recv_sem, after)
    rim_copy.start()

    def send_one(src, dst, which, peer):
        to_next(src.at[peer], dst.at[me], out_sem.at[which], in_sem.at[which], peer).start()

    def keep(src, dst):
        dst[pl.ds(me, 1)] = src[pl.ds(me, 1)]

    def scatter(src, dst, which):
        for step in STEPS:
            send_one(src, dst, which, (me + step) % PEERS)
        keep(src, dst)

    def settle(ref, sem):
        part = ref.at[pl.ds(0, PEERS - 1)]
        pltpu.make_async_copy(part, part, sem).wait()

    loads[6].wait()
    for p in range(PEERS):
        send_h[p] = filt_ref[HELD * p : HELD * p + HELD]
    scatter(send_h, recv_h, 0)
    loads[1].wait()
    kv_copies = [
        to_next(src, kv_in.at[n], kv_send_sem.at[n], kv_recv_sem.at[n], after)
        for n, src in enumerate((k_ref, v_ref))
    ]
    kv_copies[0].start()

    rim_copy.wait_recv()
    for n in range(3):
        leading = rim_in[n * RIM : (n + 1) * RIM].astype(F32)
        ext[n, 0:RIM] = jnp.where(me > 0, leading, 0.0)

    short[0, 0:8] = short_conv(0, 8, slice(None))

    mine = me // 4

    def by_chunk(compute, src, dst, which):
        def chunk_at(step):
            return (mine + 4 + ((step + 1) // 2) * (1 - 2 * (step % 2))) % 8

        @pl.loop(0, 7)
        def _(step):
            chunk = chunk_at(step)
            compute(chunk)
            for n in range(4):
                send_one(src, dst, which, chunk * 4 + n)

        compute(mine)
        for n in range(1, 4):
            send_one(src, dst, which, mine * 4 + (me + n) % 4)
        keep(src, dst)

    def blocks_of(wide):
        return wide.T.astype(BF16).reshape(4, NARROW, ROWS)

    def delta_chunk(chunk):
        lanes = pl.ds(pl.multiple_of(chunk * 128, 128), 128)
        send_g[pl.ds(chunk * 4, 4)] = blocks_of(up_ref[:, lanes].astype(F32) * short[0, :, lanes])

    def mixed_chunk(chunk):
        lanes = pl.ds(pl.multiple_of(chunk * 128, 128), 128)
        for n in (1, 2):
            short[n, :, lanes] = short_conv(n, ROWS, lanes)
        send_m[pl.ds(chunk * 4, 4)] = blocks_of(short[1, :, lanes] * short[2, :, lanes])

    loads[7].wait()
    by_chunk(delta_chunk, send_g, recv_g, 2)
    loads[2].wait()
    by_chunk(mixed_chunk, send_m, recv_m, 1)

    kv_copies[1].start()
    row_at = lax.broadcasted_iota(jnp.int32, (ROWS, ROWS), 0)
    lane_at = lax.broadcasted_iota(jnp.int32, (ROWS, ROWS), 1)
    settle(recv_h, in_sem.at[0])
    for g in range(HELD):
        weight_c[g, 128:256, 0:128] = jnp.zeros((ROWS, ROWS), BF16)
        weight_d[g, 128:256, 0:128] = jnp.zeros((ROWS, ROWS), BF16)

    def turned(block, g):
        line = jnp.broadcast_to(recv_h[block, g : g + 1], (ROWS, ROWS))
        return pltpu.roll(line, 0, 1, stride=1, stride_axis=0)

    def build(d, last):
        top = pl.multiple_of(d * 256, 256)
        carried = []
        for g in range(HELD):
            even = turned(2 * d, g)
            odd = turned(2 * d + 1, g)
            tile_even = jnp.where(lane_at >= row_at, even, last[g]).astype(BF16)
            tile_odd = jnp.where(lane_at >= row_at, odd, even).astype(BF16)
            weight_c[g, pl.ds(top, 128), 0:128] = tile_even
            weight_c[g, pl.ds(top + 128, 128), 128:256] = tile_even
            weight_c[g, pl.ds(top, 128), 128:256] = tile_odd
            weight_c[g, pl.ds(top + 384, 128), 0:128] = tile_odd
            weight_d[g, 0:128, pl.ds(top, 128)] = tile_even
            weight_d[g, 128:256, pl.ds(top + 128, 128)] = tile_even
            weight_d[g, 0:128, pl.ds(top + 128, 128)] = tile_odd
            weight_d[g, 128:256, pl.ds(top + 256, 128)] = tile_odd
            carried.append(odd)
        return tuple(carried)

    lax.fori_loop(0, SUPER, build, (jnp.zeros((ROWS, ROWS), F32),) * HELD)

    half = SUPER * GROUP

    def paired(recv, g):
        rows = recv[:, g * GROUP : (g + 1) * GROUP, :].reshape(SUPER, 2, GROUP, ROWS)
        return rows[:, 0].reshape(half, ROWS), rows[:, 1].reshape(half, ROWS)

    def spread(send, result, g):
        both = jnp.stack(
            [
                result[:, 0:ROWS].reshape(SUPER, GROUP, ROWS),
                result[:, ROWS : 2 * ROWS].reshape(SUPER, GROUP, ROWS),
            ],
            axis=1,
        )
        send[:, g * GROUP : (g + 1) * GROUP, :] = both.reshape(PEERS, GROUP, ROWS)

    settle(recv_g, in_sem.at[2])
    padded_g[half : 2 * half] = jnp.zeros((half, 2 * ROWS), BF16)
    for g in range(HELD):
        even, odd = paired(recv_g, g)
        padded_g[0:half, 0:ROWS] = even
        padded_g[0:half, ROWS : 2 * ROWS] = odd
        for d in range(SUPER):
            left_g[g, :, d * 256 : (d + 1) * 256] = padded_g[GROUP * d : half + GROUP * d]
        back = dot(left_g[g], weight_d[g, :, 0:LONG], ((1,), (1,))).astype(BF16)
        spread(send_d, back, g)
    scatter(send_d, recv_d, 4)

    settle(recv_m, in_sem.at[1])
    padded_m[0:half] = jnp.zeros((half, 2 * ROWS), BF16)
    for g in range(HELD):
        even, odd = paired(recv_m, g)
        padded_m[half : 2 * half, 0:ROWS] = even
        padded_m[half : 2 * half, ROWS : 2 * ROWS] = odd
        for d in range(SUPER):
            left_m[:, d * 256 : (d + 1) * 256] = padded_m[half - GROUP * d : 2 * half - GROUP * d]
        conv = dot(left_m[...], weight_c[g, 0:LONG], ((1,), (0,))).astype(BF16)
        spread(send_c, conv, g)
    scatter(send_c, recv_c, 3)

    reversal = (row_at + lane_at == ROWS - 1).astype(BF16)
    upper = (lane_at < row_at) | (lane_at == ROWS - 1)
    for g in range(HELD):
        turned_m = jnp.concatenate(
            [dot(reversal, part, ((1,), (1,))).astype(BF16) for part in paired(recv_m, g)], 0
        )
        gram[:, 0:LONG] = dot(turned_m, left_g[g], ((1,), (0,)))
        gram[:, LONG : LONG + 2 * ROWS] = jnp.zeros((2 * ROWS, 2 * ROWS), F32)

        def slid(e):
            at = pl.multiple_of(e * ROWS, ROWS)
            tile = gram[0:ROWS, pl.ds(at, ROWS)] + gram[ROWS : 2 * ROWS, pl.ds(at + ROWS, ROWS)]
            return pltpu.roll(tile, 0, 1, stride=1, stride_axis=0)

        @pl.loop(0, PEERS // 4)
        def _(quad, slid=slid):
            tiles = [slid(quad * 4 + n) for n in range(5)]
            for n in range(4):
                merged = jnp.where(upper, tiles[n], tiles[n + 1])
                raw_rows[quad * 4 + n] = jnp.sum(merged.reshape(16, 8, ROWS), axis=0)

        raw = pltpu.roll(jnp.sum(raw_rows[...], axis=1), 1, 1)
        squares = jnp.sum(raw * raw, 0, keepdims=True)
        send_f[:, g : g + 1, :] = raw.reshape(PEERS, 1, ROWS)
        send_f[:, HELD + g : HELD + g + 1, :] = jnp.broadcast_to(
            squares.reshape(1, 1, ROWS), (PEERS, 1, ROWS)
        )
    scatter(send_f, recv_f, 5)

    def follow(n, source):
        def chunk_step(chunk):
            lanes = pl.ds(pl.multiple_of(chunk * 128, 128), 128)
            part = source[pl.ds(chunk * 4, 4)].reshape(4 * NARROW, ROWS).astype(F32).T
            if n == 0:
                grads = ((0, up_ref[:, lanes].astype(F32) * part),)
            else:
                grads = ((1, part * short[2, :, lanes]), (2, part * short[1, :, lanes]))
            for which, grad in grads:
                ext[which, 0:ROWS, lanes] = grad
                edge_out[which, :, lanes] = grad[0:RIM].astype(BF16)

        @pl.loop(0, CHANNELS // 256)
        def _(pair):
            chunk_step(2 * pair)
            chunk_step(2 * pair + 1)

    def edge_copy(n):
        part = pl.ds(0, 1) if n == 0 else pl.ds(1, 2)
        return to_next(
            edge_out.at[part],
            edge_in.at[part],
            edge_send_sem.at[n],
            edge_recv_sem.at[n],
            before,
        )

    def trail(n):
        trailing = edge_in[n].astype(F32)
        ext[n, ROWS : ROWS + RIM] = jnp.where(me < PEERS - 1, trailing, 0.0)

    settle(recv_d, in_sem.at[4])
    follow(1, recv_d)
    edge_copy(1).start()

    for copy in kv_copies:
        copy.wait_recv()
    query_at = lax.broadcasted_iota(jnp.int32, (ROWS, 2 * ROWS), 0)
    key_at = lax.broadcasted_iota(jnp.int32, (ROWS, 2 * ROWS), 1) - ROWS
    first = jnp.where(me > 0, -ROWS, 0)
    allowed = (key_at <= query_at) & (key_at >= first)

    loads[0].wait()

    def attend(head):
        lanes = pl.ds(pl.multiple_of(head * HEAD_DIM, HEAD_DIM), HEAD_DIM)
        keys = jnp.concatenate([kv_in[0, :, lanes], k_ref[:, lanes]], 0)
        values = jnp.concatenate([kv_in[1, :, lanes], v_ref[:, lanes]], 0)
        scores = dot(q_ref[:, lanes], keys, ((1,), (1,))) * (1.0 / math.sqrt(HEAD_DIM))
        masked = jnp.where(allowed, scores, -jnp.inf)
        largest = jnp.max(masked, axis=1, keepdims=True)
        raised = jnp.exp(masked - largest)
        weights = (raised / jnp.sum(raised, axis=1, keepdims=True)).astype(BF16)
        att_ref[:, lanes] = dot(weights, values, ((1,), (0,))).astype(BF16)

    @pl.loop(0, CHANNELS // HEAD_DIM // 2)
    def _(pair):
        attend(2 * pair)
        attend(2 * pair + 1)


    settle(recv_f, in_sem.at[5])
    squares = jnp.sum(recv_f[:, HELD : 2 * HELD, :], axis=0)
    squares = jnp.sum(squares, axis=0, keepdims=True)
    send_n[...] = jnp.broadcast_to(squares, (8, ROWS))

    def norm_copy(step):
        return pltpu.make_async_remote_copy(
            src_ref=send_n,
            dst_ref=recv_n.at[tp],
            send_sem=out_sem.at[6],
            recv_sem=in_sem.at[6],
            device_id=(me, (tp + step) % TPS),
            device_id_type=MESH,
        )

    for step in range(1, TPS):
        norm_copy(step).start()
    recv_n[pl.ds(tp, 1)] = send_n[...].reshape(1, 8, ROWS)
    for p in range(PEERS):
        raw_ref[HELD * p : HELD * p + HELD] = recv_f[p, 0:HELD]

    settle(recv_c, in_sem.at[3])
    follow(0, recv_c)
    edge_copy(0).start()
    edge_copy(1).wait_recv()
    trail(1)
    trail(2)

    @pl.loop(0, CHANNELS // 128)
    def _(chunk):
        lanes = pl.ds(pl.multiple_of(chunk * 128, 128), 128)
        kg_ref[:, lanes] = anti_short(ext, taps_ref, 1, lanes)
        vg_ref[:, lanes] = anti_short(ext, taps_ref, 2, lanes)

    part = recv_n.at[pl.ds(0, TPS - 1)]
    pltpu.make_async_copy(part, part, in_sem.at[6]).wait()
    total = jnp.sum(recv_n[:, 0, :], axis=0, keepdims=True)
    total = jnp.sum(total, axis=1, keepdims=True)
    factor = jnp.minimum(1.0, math.sqrt(TOTAL) / jnp.sqrt(total))
    factor_ref[...] = jnp.broadcast_to(factor, (8, ROWS))


    edge_copy(0).wait_recv()
    trail(0)

    rim_copy.wait_send()
    for copy in kv_copies:
        copy.wait_send()
    for n in range(2):
        edge_copy(n).wait_send()
    for n, ref in enumerate((send_h, send_m, send_g, send_c, send_d, send_f)):
        settle(ref, out_sem.at[n])
    pltpu.make_async_copy(part, part, out_sem.at[6]).wait()


def anti_short(ext, taps_ref, n, lanes):
    total = taps_ref[n, 0:1, lanes] * ext[n, 0:ROWS, lanes]
    for s in range(1, SHORT):
        total += taps_ref[n, s : s + 1, lanes] * ext[n, s : s + ROWS, lanes]
    return total.astype(BF16)


def finish_kernel(
    ext, taps_ref, att, kg, vg, raw_ref, factor_ref, att_hbm, qg_hbm, kg_hbm, vg_hbm, fg_hbm,
    fg_ref, grads, sems
):
    copies = [
        pltpu.make_async_copy(att, att_hbm, sems.at[0]),
        pltpu.make_async_copy(kg, kg_hbm, sems.at[1]),
        pltpu.make_async_copy(vg, vg_hbm, sems.at[2]),
        pltpu.make_async_copy(fg_ref, fg_hbm, sems.at[3]),
    ]
    for copy in copies[:3]:
        copy.start()
    fg_ref[...] = raw_ref[...] * factor_ref[0:1]
    copies[3].start()
    for part in range(4):
        for step in range(2):
            lanes = slice(part * 256 + step * 128, part * 256 + step * 128 + 128)
            grads[:, lanes] = anti_short(ext, taps_ref, 0, lanes)
        lanes = slice(part * 256, part * 256 + 256)
        copies.append(
            pltpu.make_async_copy(grads.at[:, lanes], qg_hbm.at[:, lanes], sems.at[4 + part])
        )
        copies[-1].start()
    for copy in copies:
        copy.wait()


def finish(*args):
    wide = jax.ShapeDtypeStruct((ROWS, CHANNELS), BF16)
    vmem = pl.BlockSpec(memory_space=pltpu.VMEM)
    return pl.pallas_call(
        finish_kernel,
        out_shape=(wide, wide, wide, wide, jax.ShapeDtypeStruct((64, ROWS), F32)),
        in_specs=[vmem] * 7,
        out_specs=(pl.BlockSpec(memory_space=pltpu.HBM),) * 5,
        scratch_shapes=[
            pltpu.VMEM((64, ROWS), F32),
            pltpu.VMEM((ROWS, CHANNELS), BF16),
            pltpu.SemaphoreType.DMA((8,)),
        ],
        compiler_params=pltpu.CompilerParams(vmem_limit_bytes=6 * 1024 * 1024),
    )(*args)


def on_device(*args):
    vmem = pl.BlockSpec(memory_space=pltpu.VMEM)
    anywhere = pl.BlockSpec(memory_space=pltpu.HBM)
    own = pltpu.VMEM((ROWS, CHANNELS), BF16)
    wide = jax.ShapeDtypeStruct((ROWS, CHANNELS), BF16)
    exchanged = pltpu.VMEM((PEERS, NARROW, ROWS), BF16)
    half = SUPER * GROUP
    args = list(args)
    taps = args[6]
    args[7] = args[7].T
    args = [pltpu.with_memory_space_constraint(arg, pltpu.HBM) for arg in args]
    att, kg, vg, ext, raw, factor = pl.pallas_call(
        kernel,
        out_shape=(
            wide,
            wide,
            wide,
            jax.ShapeDtypeStruct((3, ROWS + RIM, CHANNELS), F32),
            jax.ShapeDtypeStruct((64, ROWS), F32),
            jax.ShapeDtypeStruct((8, ROWS), F32),
        ),
        in_specs=[anywhere] * 9,
        out_specs=(vmem,) * 6,
        scratch_shapes=[
            *[own] * 6,
            pltpu.VMEM((3, SHORT, CHANNELS), F32),
            pltpu.VMEM((64, ROWS), F32),
            own,
            pltpu.SemaphoreType.DMA((INPUTS,)),
            pltpu.VMEM((3 * RIM, CHANNELS), BF16),
            pltpu.VMEM((3 * RIM, CHANNELS), BF16),
            pltpu.VMEM((2, ROWS, CHANNELS), BF16),
            pltpu.VMEM((3, ROWS, CHANNELS), F32),
            pltpu.VMEM((PEERS, HELD, ROWS), F32),
            pltpu.VMEM((PEERS, HELD, ROWS), F32),
            *[exchanged] * 8,
            pltpu.VMEM((PEERS, 2 * HELD, ROWS), F32),
            pltpu.VMEM((PEERS, 2 * HELD, ROWS), F32),
            pltpu.VMEM((8, ROWS), F32),
            pltpu.VMEM((TPS, 8, ROWS), F32),
            pltpu.VMEM((3, RIM, CHANNELS), BF16),
            pltpu.VMEM((3, RIM, CHANNELS), BF16),
            pltpu.VMEM((PEERS, 8, ROWS), F32),
            pltpu.VMEM((2 * half, 2 * ROWS), BF16),
            pltpu.VMEM((2 * half, 2 * ROWS), BF16),
            pltpu.VMEM((half, LONG), BF16),
            pltpu.VMEM((HELD, half, LONG), BF16),
            pltpu.VMEM((HELD, LONG + 256, 256), BF16),
            pltpu.VMEM((HELD, 256, LONG + 128), BF16),
            pltpu.VMEM((2 * ROWS, LONG + 2 * ROWS), F32),
            pltpu.SemaphoreType.DMA,
            pltpu.SemaphoreType.DMA,
            pltpu.SemaphoreType.DMA((2,)),
            pltpu.SemaphoreType.DMA((2,)),
            pltpu.SemaphoreType.DMA((7,)),
            pltpu.SemaphoreType.DMA((7,)),
            pltpu.SemaphoreType.DMA((2,)),
            pltpu.SemaphoreType.DMA((2,)),
        ],
        compiler_params=pltpu.CompilerParams(
            collective_id=0, has_side_effects=True, vmem_limit_bytes=32 * 1024 * 1024
        ),
        cost_estimate=pl.CostEstimate(
            flops=3_400_000_000, bytes_accessed=4_000_000, transcendentals=300_000
        ),
    )(*args)
    outs = finish(ext, taps, att, kg, vg, raw, factor)
    return (*outs[:4], outs[4].T)


def solution(mesh):
    wide = P("ctx", "tp")
    in_specs = (wide,) * 6 + (P(None, None, "tp"), wide, wide)
    return jax.shard_map(
        on_device, mesh=mesh, in_specs=in_specs, out_specs=(wide,) * 5, check_vma=False
    )
```
